32 devices in a mesh: facet: 4 (over z), vis: 8 (over y, x, core).
Axes of the slice: x: 2, y: 2, z: 4, core: 2. Of those that a mesh axis runs over, the one named last changes fastest.
Arguments:
- vis_obs: float32 [4096, 2, 4, 1024], P(('facet', 'vis')), may hold values from -6 to 6
- uv_coords: float32 [4096, 2, 1024], P(('facet', 'vis')), may hold values from -16 to 16
- vis_weight: float32 [4096, 1024], P(('facet', 'vis')), may hold values from 0.5 to 900, as said below
- block_group: int32 [4096, 1], P(('facet', 'vis')), may hold values from 0 to 31; in each aligned block of 128 rows (0 to 127, 128 to 255, ...) at most 8 rows name the same one
- tile_slot: int32 [4096], P(('facet', 'vis')), may hold values from 0 to 63
- w_plane: int32 [4096], P(('facet', 'vis')), may hold values from 0 to 31
- model_tiles: bfloat16 [2048, 2, 32, 128], P(('facet', 'vis')), may hold values from -6 to 6
- w_kernels: bfloat16 [32, 2, 32, 32], replicated, may hold values from -0.75 to 0.75
Outputs:
- residual_vis: float32 [4096, 2, 4, 1024], P(('facet', 'vis'))
- residual_tiles: float32 [2048, 2, 32, 128], P(('facet', 'vis'))
The draws below stay inside these ranges and needn't reach their ends.
Inputs may be any that keep to these rules, and one draw needn't show every extreme that they name: `block_group`: in the 128 rows of one device (aligned blocks of 128 rows) no group is named by more than 8 rows, a bound that some block reaches. `vis_weight`: Positive.
All inputs are finite; a program needn't handle non-finite values.
Results may differ from the reference program's by a relative error of at most 0.0045.
Values may be sent and summed in bfloat16 or wider, within the bound.
No kernel may reach another device: no remote copies, remote signals or barrier semaphores. Data moves between devices by JAX's collectives and lax.ppermute only.
A program may use at most 128 MiB of HBM per device.

```python
import math
import jax
import jax.numpy as jnp
import numpy as np
from jax import lax

S = 32
P_SIZE = 4
NVIS = 1024
WPLANES = 32
BLK_DEV = 128
TILE_DEV = 64
GROUPS = 32
CAP = 8
NBLK = 4096
NTILES = 2048


def draw_vis_weight(key, part):
    key_rows = jax.random.fold_in(key, 11)
    key_columns = jax.random.fold_in(key, 12)
    key_entries = jax.random.fold_in(key, 13)
    position = jnp.arange(NBLK, dtype=jnp.float32)[:, None] / max(NBLK - 1, 1)
    row_scale = jnp.exp(jax.random.uniform(key_rows, (NBLK, 1), jnp.float32, 0.0, math.log(10.0)))
    column_scale = jnp.exp(jax.random.uniform(key_columns, (1, NVIS), jnp.float32, 0.0, math.log(10.0)))
    fine_scale = jax.random.uniform(key_entries, (NBLK, NVIS), jnp.float32, 0.5, 1.0)
    ramp_scale = 1.0 + 2.0 * position
    return (ramp_scale * row_scale * column_scale * fine_scale).astype(jnp.float32)


def touch_ends(array, rng, low, largest):
    index_at = [jax.random.randint(jax.random.fold_in(rng, axis), (), 0, length) for axis, length in enumerate(array.shape)]
    widest = array.shape.index(max(array.shape))
    beside = index_at[:widest] + [(index_at[widest] + 1) % array.shape[widest]] + index_at[widest + 1:]
    return array.at[tuple(index_at)].set(low).at[tuple(beside)].set(largest)


def level_of(key, extent, split, low, largest):
    gain, own = 1.0, jax.random.fold_in(key, 6)
    for dim, blocks in split:
        steps = jnp.exp(jax.random.uniform(jax.random.fold_in(own, dim), (blocks,), jnp.float32, low / len(split), largest / len(split)))
        gain = gain * jnp.repeat(steps, extent[dim] // blocks).reshape([-1 if axis == dim else 1 for axis in range(len(extent))])
    return gain


def deal_out(own_key, own, number, rows, number_of, top, bound, slope):
    ranking = jax.random.permutation(own_key, number_of)
    packed, ordinary = load_shares(number_of, rows * top, bound, slope, True), load_shares(number_of, rows * top, bound, slope, False)
    places = jnp.arange(number_of)

    def named(lengths, turn):
        used = int((lengths > 0).sum())
        fixed = max(1, used // 4)
        shifted = fixed + (places - fixed + turn * (used - fixed)) % max(1, number_of - fixed)
        return jnp.zeros((number_of,), jnp.int32).at[ranking[jnp.where(places < fixed, places, shifted)]].set(jnp.asarray(lengths, jnp.int32))

    lengths = jnp.where(number % 4 == 0, named(packed, number // 4), named(ordinary, number - number // 4 - 1))
    mixed = jax.random.permutation(jax.random.fold_in(own, 3), number_of)
    source_of, sink = mixed[0:number_of // 2 * 2:2], mixed[1:number_of // 2 * 2:2]
    slack = jnp.minimum(lengths[source_of] - 1, bound - lengths[sink]) // 2
    slack = jnp.where((source_of == ranking[0]) | (sink == ranking[0]) | (lengths[sink] == 0), 0, jnp.maximum(slack, 0))
    shifted = jax.random.randint(jax.random.fold_in(own, 4), (number_of // 2,), 0, 1 << 20) % (slack + 1)
    lengths = lengths.at[source_of].add(-shifted).at[sink].add(shifted)
    items = jnp.searchsorted(jnp.cumsum(lengths), jnp.arange(rows * top), side="right").astype(jnp.int32)
    table = items.reshape(top, rows).T
    table = table[jax.random.permutation(jax.random.fold_in(own, 1), rows)]
    turn = jax.random.randint(jax.random.fold_in(own, 2), (rows, 1), 0, top)
    return jnp.take_along_axis(table, (jnp.arange(top)[None, :] + turn) % top, axis=1)


def load_shares(amount, total, bound, slope, full):
    weights = [(1 << 20) // math.isqrt(grade ** slope) + 1 for grade in range(1, amount + 1)]
    largest = bound if full else min(bound, max(-(-total // amount), total * weights[0] // sum(weights)))
    least = 1 if total - largest >= amount - 1 else 0
    counts, spare = [largest] + [least] * (amount - 1), total - largest - least * (amount - 1)
    while spare > 0:
        candidates = [i for i in range(1, amount) if counts[i] < largest] or [i for i in range(1, amount) if counts[i] < bound]
        pool, budget = sum([weights[i] for i in candidates]), spare
        for i in candidates:
            more = min(bound - counts[i], max(1, budget * weights[i] // pool), spare)
            counts[i] = counts[i] + more
            spare = spare - more
    return np.array(counts)


def noise(own_key, extent, width, limit, pieces=(), kind=jnp.bfloat16):
    entries = jax.random.normal(own_key, extent, jnp.float32) * width
    if len(pieces) > 0:
        entries = level_of(own_key, extent, pieces, -0.22, 0.18) * entries
    return jnp.clip(entries, min=-limit, max=limit).astype(kind)


def setup_inputs(seed: int = 0) -> dict:
    key_of = jax.random.split(jax.random.key(seed), 9)
    vis_obs = noise(key_of[0], (NBLK, 2, P_SIZE, NVIS), 1.0, 6.0, ((0, 32),), jnp.float32)
    uv_coords = jnp.clip(jax.random.uniform(key_of[1], (NBLK, 2, NVIS), jnp.float32, -16.0, 16.0) * level_of(key_of[1], (NBLK, 2, NVIS), ((0, 32),), -0.4, 0.0), -16.0, 16.0)
    vis_weight = draw_vis_weight(jax.random.fold_in(key_of[8], 71), 0)
    block_group_keys = jax.random.split(jax.random.fold_in(key_of[3], 1), NBLK // BLK_DEV)
    block_group_turns = jax.random.permutation(jax.random.fold_in(key_of[3], 3), NBLK // BLK_DEV)
    block_group = jax.vmap(lambda own, number: deal_out(jax.random.fold_in(key_of[3], 2), own, number, BLK_DEV, GROUPS, 1, CAP, 2))(block_group_keys, block_group_turns).reshape((NBLK, 1))
    tile_slot = touch_ends(jax.random.randint(key_of[4], (NBLK,), 0, TILE_DEV), jax.random.fold_in(key_of[4], 1), 0, TILE_DEV - 1).astype(jnp.int32)
    w_plane = touch_ends(jax.random.randint(key_of[5], (NBLK,), 0, WPLANES), jax.random.fold_in(key_of[5], 1), 0, WPLANES - 1).astype(jnp.int32)
    model_tiles = noise(key_of[6], (NTILES, 2, S, P_SIZE * S), 1.0, 6.0, ((0, 32),))
    w_kernels = noise(key_of[7], (WPLANES, 2, S, S), (2 * S) ** -0.5, 0.75)
    return {"vis_obs": vis_obs, "uv_coords": uv_coords, "vis_weight": vis_weight, "block_group": block_group, "tile_slot": tile_slot, "w_plane": w_plane, "model_tiles": model_tiles, "w_kernels": w_kernels}


def rounded(operand):
    return lax.optimization_barrier(operand.astype(jnp.bfloat16))


def complex_product(form_text, left_side, right_side):
    left_side = left_side.astype(jnp.float32)
    right_side = right_side.astype(jnp.float32)
    real_part = jnp.einsum(form_text, left_side[:, 0], right_side[:, 0]) - jnp.einsum(form_text, left_side[:, 1], right_side[:, 1])
    imag_part = jnp.einsum(form_text, left_side[:, 0], right_side[:, 1]) + jnp.einsum(form_text, left_side[:, 1], right_side[:, 0])
    return jnp.stack((real_part, imag_part), axis=1)


def conjugate(operand):
    return jnp.stack((operand[:, 0], -operand[:, 1]), axis=1)


def phasors(coordinates, sub_width):
    offsets = (jnp.arange(sub_width) - sub_width // 2).astype(jnp.float32) * (-2.0 * math.pi / sub_width)
    angles = coordinates[:, :, None, :] * offsets[None, None, :, None]
    return jnp.cos(angles), jnp.sin(angles)


def degrid_grid(tile_rows, kernels, coordinates, observed, weights):
    block_count = tile_rows.shape[0]
    sub_width = tile_rows.shape[2]
    span_width = tile_rows.shape[3]
    pol_count = span_width // sub_width
    vis_count = coordinates.shape[-1]
    left_prod = rounded(complex_product("nij,njq->niq", kernels, tile_rows))
    left_prod = left_prod.reshape(block_count, 2, sub_width, pol_count, sub_width)
    kerneled = rounded(complex_product("nlpm,nkm->nlpk", left_prod, kernels).reshape(block_count, 2, sub_width, span_width))
    cosine, sine_part = phasors(coordinates, sub_width)
    along_u = rounded(jnp.stack((cosine[:, 0], sine_part[:, 0]), axis=1))
    phase_real = cosine[:, 1][:, None]
    phase_imag = sine_part[:, 1][:, None]
    spread = complex_product("nlq,nlk->nqk", kerneled, along_u).reshape(block_count, 2, pol_count, sub_width, vis_count)
    predicted_real = jnp.sum(spread[:, 0] * phase_real - spread[:, 1] * phase_imag, axis=2) / sub_width
    predicted_imag = jnp.sum(spread[:, 0] * phase_imag + spread[:, 1] * phase_real, axis=2) / sub_width
    residual = observed - jnp.stack((predicted_real, predicted_imag), axis=1)
    factor = (weights / sub_width)[:, None, None, :]
    residual_real = residual[:, 0][:, :, None, :]
    residual_imag = residual[:, 1][:, :, None, :]
    weighted_real = (residual_real * phase_real + residual_imag * phase_imag) * factor
    weighted_imag = (residual_imag * phase_real - residual_real * phase_imag) * factor
    weighted = rounded(jnp.stack((weighted_real, weighted_imag), axis=1).reshape(block_count, 2, span_width, vis_count))
    gridded = rounded(complex_product("nlk,nqk->nlq", conjugate(along_u), weighted))
    back_prod = rounded(complex_product("nji,njq->niq", conjugate(kernels), gridded))
    back_prod = back_prod.reshape(block_count, 2, sub_width, pol_count, sub_width)
    contribution = complex_product("nlpm,nmk->nlpk", back_prod, conjugate(kernels)).reshape(block_count, 2, sub_width, span_width)
    return residual, contribution


def reference(vis_obs, uv_coords, vis_weight, block_group, tile_slot, w_plane, model_tiles, w_kernels):
    block_count = vis_obs.shape[0]
    batch_size = math.gcd(block_count, 64)
    tile_index = (block_group[:, 0] * TILE_DEV + tile_slot).astype(jnp.int32)

    def split_blocks(operand):
        return operand.reshape((block_count // batch_size, batch_size) + operand.shape[1:])

    def process(inputs):
        index_part, plane_part, coord_part, observed, weights = inputs
        tile_rows = jnp.take(model_tiles, index_part, axis=0)
        kernels = jnp.take(w_kernels, plane_part, axis=0)
        return degrid_grid(tile_rows, kernels, coord_part, observed, weights)

    residual, contribution = lax.map(process, (split_blocks(tile_index), split_blocks(w_plane), split_blocks(uv_coords), split_blocks(vis_obs), split_blocks(vis_weight)))
    residual = residual.reshape(vis_obs.shape)
    contribution = contribution.reshape((block_count,) + model_tiles.shape[1:])
    summed = jax.ops.segment_sum(contribution, tile_index, num_segments=model_tiles.shape[0])
    weight_sum = jnp.sum(vis_weight)
    scaling = (block_count * vis_obs.shape[-1]) / weight_sum
    return residual, summed * scaling
```

```python
import functools
import math

import jax
import jax.numpy as jnp
from jax import lax
from jax.experimental import pallas as pl
from jax.experimental.pallas import tpu as pltpu
from jax.sharding import PartitionSpec as P

AXES = ("facet", "vis")
BATCH = 8
LANES = 256
TILE = 128
SIN_TERMS = [(-1.0) ** i * (2.0 * math.pi) ** (2 * i + 1) / math.factorial(2 * i + 1) for i in range(8)]
COS_TERMS = [(-1.0) ** i * (2.0 * math.pi) ** (2 * i) / math.factorial(2 * i) for i in range(9)]


def polynomial(terms, square):
    total = jnp.full_like(square, terms[-1])
    for term in terms[-2::-1]:
        total = total * square + term
    return total


def unit_phasor(turns):
    halves = jnp.floor(turns * 2.0 + 0.5)
    part = turns - halves * 0.5
    odd = halves - 2.0 * jnp.floor(halves * 0.5)
    sign = 1.0 - 2.0 * odd
    square = part * part
    return sign * polynomial(COS_TERMS, square), -sign * part * polynomial(SIN_TERMS, square)


def phasor_powers(cosine, sine, count):
    powers = {1: (cosine, sine)}
    for j in range(2, count + 1):
        ar, ai = powers[j // 2]
        br, bi = powers[j - j // 2]
        if j % 2 == 0:
            powers[j] = (ar * ar - ai * ai, 2.0 * ar * ai)
        else:
            powers[j] = (ar * br - ai * bi, ar * bi + ai * br)
    return powers


def rows_dot(left, right, left_dim, right_dim):
    return lax.dot_general(
        left, right, (((left_dim,), (right_dim,)), ((), ())), preferred_element_type=jnp.float32
    )


def split(value):
    high = value.astype(jnp.bfloat16)
    return high, (value - high.astype(jnp.float32)).astype(jnp.bfloat16)


def block_kernel(
    meta, order, slot, plane, tile_ref, obs_ref, u_ref, v_ref, w_ref, left_ref, back_ref, right_ref, *rest, aliased
):
    if aliased:
        old_ref, res_ref, con_ref, fu_ref, fv_ref = rest
    else:
        res_ref, con_ref, fu_ref, fv_ref = rest
    half = fv_ref.shape[0] // 2 - 1
    width = 2 * half
    pols = obs_ref.shape[2]
    step = pl.program_id(0)
    inside = lax.rem(step, BATCH)

    @pl.when((inside == 0) & (step < meta[1]))
    def _():
        cosine, sine = unit_phasor(u_ref[...] * (1.0 / width))
        powers = phasor_powers(cosine, sine, half)
        ones, zeros = jnp.ones_like(cosine), jnp.zeros_like(cosine)
        stride = 2 * width

        def put(row, value):
            for t in range(fu_ref.shape[0]):
                fu_ref[t, pl.ds(row, BATCH, stride=stride), :] = value[:, t * TILE : (t + 1) * TILE]

        put(0, ones)
        put(width, zeros)
        for j in range(1, half + 1):
            real, imag = powers[j]
            if j < half:
                put(j, real)
                put(width + j, imag)
            low = half if j == half else half + j
            put(low, real)
            put(width + low, -imag)
        cosine, sine = unit_phasor(v_ref[...] * (1.0 / width))
        powers = phasor_powers(cosine, sine, half)
        for j in range(1, half + 1):
            fv_ref[j], fv_ref[half + 1 + j] = powers[j]

    which = plane[order[meta[0] + step]]

    def work():
        lane = lax.broadcasted_iota(jnp.int32, (2 * width, pols * width), 1)
        unpaired = lane < 2 * pols
        wide = 2 * pols * width
        band = lax.rem(lax.broadcasted_iota(jnp.int32, (width, wide), 1), pols)

        def paired(full):
            first, second = full[:, : pols * width], full[:, pols * width :]
            total = jnp.where(unpaired, first, first + second)
            change = jnp.where(unpaired, second, first - second)
            return jnp.concatenate([total, change], axis=1)

        spread_kernel = right_ref[which]
        right = jnp.concatenate(
            [
                jnp.where(band == p, spread_kernel[r * width : (r + 1) * width], jnp.zeros((), jnp.bfloat16))
                for r in range(2)
                for p in range(pols)
            ],
            axis=0,
        )
        tile = tile_ref[0].reshape(2 * width, pols * width)
        left = rows_dot(left_ref[which], tile, 1, 0).astype(jnp.bfloat16)
        left_real, left_imag = left[:width], left[width:]
        left = jnp.concatenate(
            [jnp.concatenate([left_real, left_imag], axis=1), jnp.concatenate([-left_imag, left_real], axis=1)],
            axis=0,
        )
        model = paired(rows_dot(left, right, 1, 0)).astype(jnp.bfloat16)
        base = pl.multiple_of(inside * 2 * width, 2 * width)
        sublane = lax.broadcasted_iota(jnp.int32, (2 * pols, LANES), 0)
        turn = jnp.where(sublane < pols, -1.0, 1.0)
        gridded = None
        for start in range(0, u_ref.shape[1], LANES):
            lanes = pl.ds(start, LANES)
            along_u = jnp.concatenate(
                [fu_ref[start // TILE + t, pl.ds(base, 2 * width), :] for t in range(LANES // TILE)], axis=1
            ).astype(jnp.bfloat16)
            spread = rows_dot(model, along_u, 0, 0).reshape(width, 2 * pols, LANES)

            def phase(index):
                return jnp.broadcast_to(fv_ref[index, pl.ds(inside, 1), lanes], (2 * pols, LANES))

            cos_part = spread[0] + spread[half] * phase(half)
            sin_part = -spread[half] * phase(2 * half + 1)
            for j in range(1, half):
                cos_part = cos_part + spread[j] * phase(j)
                sin_part = sin_part + spread[half + j] * phase(half + 1 + j)
            predicted = cos_part + turn * jnp.roll(sin_part, pols, axis=0)
            observed = jnp.concatenate([obs_ref[0, 0, :, lanes], obs_ref[0, 1, :, lanes]], axis=0)
            residual = observed - predicted * (1.0 / width)
            res_ref[0, 0, :, lanes] = residual[:pols]
            res_ref[0, 1, :, lanes] = residual[pols:]
            scaled = residual * (w_ref[pl.ds(inside, 1), lanes] * (1.0 / width))
            turned = -turn * jnp.roll(scaled, pols, axis=0)
            cos_rows, sin_rows = [scaled], [scaled * phase(half) - turned * phase(2 * half + 1)]
            for j in range(1, half):
                cos_rows.append(scaled * phase(j))
                sin_rows.append(turned * phase(half + 1 + j))
            weighted = jnp.concatenate(cos_rows + sin_rows, axis=0).astype(jnp.bfloat16)
            part = rows_dot(along_u, weighted, 1, 1)
            gridded = part if gridded is None else gridded + part
        back = rows_dot(jnp.concatenate(split(paired(gridded)), axis=0), right, 1, 1)
        back = back[: 2 * width] + back[2 * width :]
        span = pols * width
        back_real = back[:width, :span] + back[width:, span:]
        back_imag = back[:width, span:] - back[width:, :span]
        back = jnp.concatenate([back_real, back_imag], axis=0)
        result = rows_dot(back_ref[which], jnp.concatenate(split(back), axis=1), 1, 0)
        result = result[:, :span] + result[:, span:]
        con_ref[0] = result.astype(con_ref.dtype).reshape(con_ref.shape[1:])

    pl.when(step < meta[1])(work)
    if aliased:

        @pl.when((step >= meta[1]) & (step == 0))
        def _():
            res_ref[...] = old_ref[...]
            con_ref[...] = jnp.zeros_like(con_ref)


def process_blocks(steps, base, count, order, slot, plane, tiles, observed, u, v, weight, left, back, right, old=None):
    pols, vis_count = observed.shape[2:]
    width = tiles.shape[2]
    aliased = old is not None
    meta = jnp.stack([base, count]).astype(jnp.int32)

    def item(i, meta):
        return meta[0] + jnp.minimum(i, jnp.maximum(meta[1] - 1, 0))

    def by_block(i, meta, order, slot, plane):
        return (order[item(i, meta)], 0, 0, 0)

    def by_slot(i, meta, order, slot, plane):
        return (slot[order[item(i, meta)]], 0, 0, 0)

    def by_batch(i, meta, order, slot, plane):
        return (lax.div(item(i, meta), BATCH), 0)

    def whole(i, meta, order, slot, plane):
        return (0, 0, 0)

    tile_spec = pl.BlockSpec((1,) + tiles.shape[1:], by_slot)
    vis_spec = pl.BlockSpec((1,) + observed.shape[1:], by_block)
    row_spec = pl.BlockSpec((BATCH, vis_count), by_batch)
    operands = [tiles, observed, u, v, weight, left, back, right]
    in_specs = [tile_spec, vis_spec, row_spec, row_spec, row_spec] + [
        pl.BlockSpec(table.shape, whole) for table in (left, back, right)
    ]
    aliases = {}
    if aliased:
        operands.append(old)
        in_specs.append(vis_spec)
        aliases = {len(operands) + 3: 0}
    return pl.pallas_call(
        functools.partial(block_kernel, aliased=aliased),
        out_shape=(
            jax.ShapeDtypeStruct(observed.shape, jnp.float32),
            jax.ShapeDtypeStruct(tiles.shape, jnp.bfloat16),
        ),
        grid_spec=pltpu.PrefetchScalarGridSpec(
            num_scalar_prefetch=4,
            grid=(steps,),
            in_specs=in_specs,
            out_specs=(vis_spec, tile_spec),
            scratch_shapes=[
                pltpu.VMEM((vis_count // TILE, BATCH * 2 * width, TILE), jnp.float32),
                pltpu.VMEM((width + 2, BATCH, vis_count), jnp.float32),
            ],
        ),
        input_output_aliases=aliases,
        compiler_params=pltpu.CompilerParams(vmem_limit_bytes=40 * 1024 * 1024),
        cost_estimate=pl.CostEstimate(
            flops=steps * 2 * 2 * 2 * width * 2 * pols * width * vis_count,
            bytes_accessed=steps * 2 * pols * vis_count * 40,
            transcendentals=0,
        ),
        name="process_blocks",
    )(meta, order, slot, plane, *operands)


def sum_kernel(requested, scale_ref, *refs, last):
    if last:
        old_ref, arrived_ref, out_ref = refs
        out_ref[...] = old_ref[...]
    else:
        arrived_ref, out_ref = refs
        out_ref[...] = jnp.zeros_like(out_ref)

    @pl.loop(0, arrived_ref.shape[0])
    def _(i):
        tile = requested[i]

        @pl.when(tile >= 0)
        def _():
            out_ref[tile] += arrived_ref[i].astype(jnp.float32)

    if last:
        out_ref[...] = out_ref[...] * scale_ref[0]


def sum_tiles(requested, scale, arrived, owned, old=None):
    shape = (owned,) + arrived.shape[1:]
    operands = [arrived] if old is None else [old, arrived]
    vmem = pl.BlockSpec(memory_space=pltpu.VMEM)
    return pl.pallas_call(
        functools.partial(sum_kernel, last=old is not None),
        out_shape=jax.ShapeDtypeStruct(shape, jnp.float32),
        in_specs=[pl.BlockSpec(memory_space=pltpu.SMEM)] * 2 + [vmem] * len(operands),
        out_specs=vmem,
        compiler_params=pltpu.CompilerParams(vmem_limit_bytes=40 * 1024 * 1024),
        cost_estimate=pl.CostEstimate(flops=arrived.size, bytes_accessed=arrived.size * 4, transcendentals=0),
        name="sum_tiles",
    )(requested, scale, *operands)


def kernel_tables(w_kernels, pols):
    planes, _, width, _ = w_kernels.shape
    half = width // 2
    real, imag = w_kernels[:, 0], w_kernels[:, 1]

    def offsets(table):
        return jnp.concatenate([table[:, half:], table[:, :1], table[:, half - 1 : 0 : -1]], axis=1)

    real_rows, imag_rows = offsets(real), offsets(imag)
    left = jnp.concatenate(
        [jnp.concatenate([real_rows, -imag_rows], axis=2), jnp.concatenate([imag_rows, real_rows], axis=2)], axis=1
    )
    back = jnp.swapaxes(left, 1, 2)
    real_columns, imag_columns = jnp.swapaxes(real_rows, 1, 2), jnp.swapaxes(imag_rows, 1, 2)
    right = jnp.concatenate(
        [
            jnp.stack([real_columns, imag_columns], axis=3),
            jnp.stack([-imag_columns, real_columns], axis=3),
        ],
        axis=1,
    )
    right = jnp.broadcast_to(right[..., None], right.shape + (pols,)).reshape(planes, 2 * width, 2 * width * pols)
    return left, back, right


def exchange(operand):
    return lax.all_to_all(operand, AXES, split_axis=0, concat_axis=0, tiled=True)


def shards(vis_obs, uv_coords, vis_weight, block_group, tile_slot, w_plane, model_tiles, w_kernels):
    blocks = vis_obs.shape[0]
    pols = vis_obs.shape[2]
    groups = lax.axis_size(AXES)
    owned = model_tiles.shape[0]
    tile_shape = model_tiles.shape[1:]
    capacity = max(2, 2 * blocks // groups)
    early = (capacity + 1) // 2
    target = block_group[:, 0]
    markers = target[:, None] == jnp.arange(groups, dtype=jnp.int32)[None, :]
    counts = markers.astype(jnp.int32)
    before = jnp.cumsum(counts, axis=0) - counts
    rank = jnp.sum(jnp.where(markers, before, 0), axis=1)
    ranks = rank[:, None] == jnp.arange(capacity, dtype=jnp.int32)[None, :]
    wanted = jnp.sum(
        jnp.where(markers[:, :, None] & ranks[:, None, :], (tile_slot + 1)[:, None, None], 0), axis=0
    )
    own_weight = jnp.broadcast_to(jnp.sum(vis_weight)[None, None], (groups, 1))
    answers = exchange(jnp.concatenate([wanted.astype(jnp.float32), own_weight], axis=1))
    requested = answers[:, :capacity].astype(jnp.int32) - 1
    weight_sum = jnp.sum(answers[:, capacity])
    scaling = blocks * groups * vis_obs.shape[-1] / weight_sum
    scaling = scaling.reshape(1)

    left, back, right = kernel_tables(w_kernels, pols)
    is_late = rank >= early
    late = is_late.astype(jnp.int32)
    early_count = blocks - jnp.sum(late)
    late_base = (early_count + BATCH - 1) // BATCH * BATCH
    item = jnp.where(is_late, late_base + jnp.cumsum(late) - 1, jnp.cumsum(1 - late) - 1)
    items = jnp.arange(blocks + BATCH, dtype=jnp.int32)
    order = jnp.sum(
        jnp.where(items[:, None] == item[None, :], jnp.arange(blocks, dtype=jnp.int32)[None, :], 0), axis=1
    )
    slot = jnp.where(is_late, target * (capacity - early) + rank - early, target * early + rank)
    u = jnp.take(uv_coords[:, 0], order, axis=0, mode="clip")
    v = jnp.take(uv_coords[:, 1], order, axis=0, mode="clip")
    weight = jnp.take(vis_weight, order, axis=0, mode="clip")

    def send_tiles(part):
        chosen = jnp.take(model_tiles, jnp.maximum(part, 0).reshape(-1), axis=0, mode="clip")
        arrived = exchange(chosen.reshape(part.shape + tile_shape))
        return arrived.reshape((-1,) + tile_shape)

    def send_back(part):
        returned = exchange(part.reshape((groups, -1) + tile_shape))
        return returned.reshape(-1, tile_shape[0] * tile_shape[1], tile_shape[2])

    first, second = requested[:, :early], requested[:, early:]
    tiles_first = send_tiles(first)
    tiles_second = send_tiles(second)
    tables = (left, back, right)
    zero = jnp.zeros((), jnp.int32)
    residual, sent_first = process_blocks(
        blocks, zero, early_count, order, slot, w_plane, tiles_first, vis_obs, u, v, weight, *tables
    )
    late_most = blocks * (capacity - early) // capacity
    residual, sent_second = process_blocks(
        late_most,
        late_base,
        blocks - early_count,
        order,
        slot,
        w_plane,
        tiles_second,
        vis_obs,
        u,
        v,
        weight,
        *tables,
        residual,
    )
    summed = sum_tiles(first.reshape(-1), scaling, send_back(sent_first), owned)
    summed = sum_tiles(second.reshape(-1), scaling, send_back(sent_second), owned, summed)
    return residual, summed.reshape(model_tiles.shape)


def solution(mesh):
    rows = P(AXES)
    in_specs = (rows,) * 7 + (P(),)
    return jax.shard_map(shards, mesh=mesh, in_specs=in_specs, out_specs=(rows, rows), check_vma=False)
```

```python
import functools
import math

import jax
import jax.numpy as jnp
from jax import lax
from jax.experimental import pallas as pl
from jax.experimental.pallas import tpu as pltpu
from jax.sharding import PartitionSpec as P

AXES = ("facet", "vis")
BATCH = 8
LANES = 512
TILE = 128
UNROLL = 4
VMEM_BYTES = 60 * 1024 * 1024
SIN_TERMS = [(-1.0) ** i * (2.0 * math.pi) ** (2 * i + 1) / math.factorial(2 * i + 1) for i in range(8)]
COS_TERMS = [(-1.0) ** i * (2.0 * math.pi) ** (2 * i) / math.factorial(2 * i) for i in range(9)]


def polynomial(terms, square):
    total = jnp.full_like(square, terms[-1])
    for term in terms[-2::-1]:
        total = total * square + term
    return total


def unit_phasor(turns):
    halves = jnp.floor(turns * 2.0 + 0.5)
    part = turns - halves * 0.5
    odd = halves - 2.0 * jnp.floor(halves * 0.5)
    sign = 1.0 - 2.0 * odd
    square = part * part
    return sign * polynomial(COS_TERMS, square), -sign * part * polynomial(SIN_TERMS, square)


def phasor_powers(cosine, sine, count):
    powers = {1: (cosine, sine)}
    for j in range(2, count + 1):
        ar, ai = powers[j // 2]
        br, bi = powers[j - j // 2]
        if j % 2 == 0:
            powers[j] = (ar * ar - ai * ai, 2.0 * ar * ai)
        else:
            powers[j] = (ar * br - ai * bi, ar * bi + ai * br)
    return powers


def rows_dot(left, right, left_dim, right_dim):
    return lax.dot_general(
        left, right, (((left_dim,), (right_dim,)), ((), ())), preferred_element_type=jnp.float32
    )


def split(value):
    high = value.astype(jnp.bfloat16)
    return high, (value - high.astype(jnp.float32)).astype(jnp.bfloat16)


def block_kernel(
    meta, order, slot, plane, tiles, observed, u_ref, v_ref, w_ref, left_ref, back_ref, right_ref, turned_ref, *rest, aliased
):
    if aliased:
        rest = rest[1:]
    res, con, fu_ref, fv_ref, tile_buf, obs_buf, model_buf, grid_buf, res_buf, con_buf, in_sems, out_sems = rest
    half = fv_ref.shape[0] // 2 - 1
    width = 2 * half
    pols = obs_buf.shape[3]
    span = pols * width
    vis_count = u_ref.shape[1]
    step = pl.program_id(0)
    base, count = meta[0], meta[1]

    def block_at(at, k):
        return order[base + jnp.minimum(at * BATCH + k, count - 1)]

    def incoming(at, k):
        block = block_at(at, k)
        turn = lax.rem(at, 2)
        return (
            pltpu.make_async_copy(tiles.at[slot[block]], tile_buf.at[turn, k], in_sems.at[0, turn, k]),
            pltpu.make_async_copy(observed.at[block], obs_buf.at[turn, k], in_sems.at[1, turn, k]),
        )

    def outgoing(at, k):
        block = block_at(at, k)
        return (
            pltpu.make_async_copy(con_buf.at[k], con.at[slot[block]], out_sems.at[0, k]),
            pltpu.make_async_copy(res_buf.at[k], res.at[block], out_sems.at[1, k]),
        )

    def start_incoming(at):
        for k in range(BATCH):
            for copy in incoming(at, k):
                copy.start()

    def make_phasors():
        cosine, sine = unit_phasor(u_ref[...] * (1.0 / width))
        powers = phasor_powers(cosine, sine, half)

        def put(row, value):
            for t in range(vis_count // TILE):
                fu_ref[t, row * BATCH : (row + 1) * BATCH, :] = value[:, t * TILE : (t + 1) * TILE]

        put(0, jnp.ones_like(cosine))
        put(width, jnp.zeros_like(cosine))
        for j in range(1, half + 1):
            real, imag = powers[j]
            if j < half:
                put(j, real)
                put(width + j, imag)
            low = half if j == half else half + j
            put(low, real)
            put(width + low, -imag)
        cosine, sine = unit_phasor(v_ref[...] * (1.0 / width))
        powers = phasor_powers(cosine, sine, half)
        for j in range(1, half + 1):
            fv_ref[j], fv_ref[half + 1 + j] = powers[j]

    wide = 2 * span
    unpaired = lax.broadcasted_iota(jnp.int32, (2 * width, span), 1) < 2 * pols

    def paired(full):
        first, second = full[:, :span], full[:, span:]
        total = jnp.where(unpaired, first, first + second)
        change = jnp.where(unpaired, second, first - second)
        return jnp.concatenate([total, change], axis=1)

    def from_right(which):
        band = lax.rem(lax.broadcasted_iota(jnp.int32, (width, wide), 1), pols)
        table = right_ref[which]
        zero = jnp.zeros((), jnp.bfloat16)
        return jnp.concatenate(
            [jnp.where(band == p, table[r * width : (r + 1) * width], zero) for r in range(2) for p in range(pols)],
            axis=0,
        )

    def make_model(k):
        which = plane[block_at(step, k)]
        tile = tile_buf[lax.rem(step, 2), k].reshape(2 * width, span)
        left = rows_dot(left_ref[which], tile, 1, 0).astype(jnp.bfloat16)
        left_real, left_imag = left[:width], left[width:]
        left = jnp.concatenate(
            [jnp.concatenate([left_real, left_imag], axis=1), jnp.concatenate([-left_imag, left_real], axis=1)],
            axis=0,
        )
        model_buf[k] = paired(rows_dot(left, from_right(which), 1, 0)).astype(jnp.bfloat16)

    turn = jnp.where(lax.broadcasted_iota(jnp.int32, (2 * pols, LANES), 0) < pols, -1.0, 1.0)

    def degrid_and_grid(k):
        model = model_buf[k]
        gridded = None
        for start in range(0, vis_count, LANES):
            lanes = pl.ds(start, LANES)
            along_u = jnp.concatenate(
                [
                    fu_ref[start // TILE + t, pl.ds(k, 2 * width, stride=BATCH), :]
                    for t in range(LANES // TILE)
                ],
                axis=1,
            ).astype(jnp.bfloat16)
            spread = rows_dot(model, along_u, 0, 0).reshape(width, 2 * pols, LANES)

            def phase(index):
                return jnp.broadcast_to(fv_ref[index, pl.ds(k, 1), lanes], (2 * pols, LANES))

            cos_part = spread[0] + spread[half] * phase(half)
            sin_part = -spread[half] * phase(2 * half + 1)
            for j in range(1, half):
                cos_part = cos_part + spread[j] * phase(j)
                sin_part = sin_part + spread[half + j] * phase(half + 1 + j)
            predicted = cos_part + turn * jnp.roll(sin_part, pols, axis=0)
            given = obs_buf[lax.rem(step, 2), k, :, :, lanes]
            residual = jnp.concatenate([given[0], given[1]], axis=0) - predicted * (1.0 / width)
            res_buf[k, 0, :, lanes] = residual[:pols]
            res_buf[k, 1, :, lanes] = residual[pols:]
            scaled = residual * (w_ref[pl.ds(k, 1), lanes] * (1.0 / width))
            turned = -turn * jnp.roll(scaled, pols, axis=0)
            cos_rows, sin_rows = [scaled], [scaled * phase(half) - turned * phase(2 * half + 1)]
            for j in range(1, half):
                cos_rows.append(scaled * phase(j))
                sin_rows.append(turned * phase(half + 1 + j))
            weighted = jnp.concatenate(cos_rows + sin_rows, axis=0).astype(jnp.bfloat16)
            part = rows_dot(along_u, weighted, 1, 1)
            gridded = part if gridded is None else gridded + part
        grid_buf[k] = gridded

    def make_contribution(k):
        which = plane[block_at(step, k)]
        back = rows_dot(jnp.concatenate(split(paired(grid_buf[k])), axis=0), turned_ref[which], 1, 0)
        back = back[: 2 * width] + back[2 * width :]
        back_real = back[:width, :span] + back[width:, span:]
        back_imag = back[:width, span:] - back[width:, :span]
        back = jnp.concatenate([back_real, back_imag], axis=0)
        result = rows_dot(back_ref[which], jnp.concatenate(split(back), axis=1), 1, 0)
        result = result[:, :span] + result[:, span:]
        con_buf[k] = result.astype(con_buf.dtype).reshape(con_buf.shape[1:])

    @pl.when(step * BATCH < count)
    def _():
        @pl.when(step == 0)
        def _():
            start_incoming(step)

        @pl.when((step + 1) * BATCH < count)
        def _():
            start_incoming(step + 1)

        make_phasors()
        for k in range(BATCH):
            for copy in incoming(step, k):
                copy.wait()
        for k in range(BATCH):
            make_model(k)

        @pl.when(step > 0)
        def _():
            for k in range(BATCH):
                for copy in outgoing(step - 1, k):
                    copy.wait()

        @pl.loop(0, BATCH // UNROLL)
        def _(i):
            for k in range(UNROLL):
                degrid_and_grid(i * UNROLL + k)

        for k in range(BATCH):
            make_contribution(k)
        last = (step + 1) * BATCH >= count
        for k in range(BATCH):

            @pl.when(step * BATCH + k < count)
            def _():
                for copy in outgoing(step, k):
                    copy.start()

        for k in range(BATCH):

            @pl.when(last & (step * BATCH + k < count))
            def _():
                for copy in outgoing(step, k):
                    copy.wait()


def process_blocks(most, base, count, order, slot, plane, tiles, observed, u, v, weight, tables, old=None):
    pols, vis_count = observed.shape[2:]
    width = tiles.shape[2]
    meta = jnp.stack([base, count]).astype(jnp.int32)

    def by_batch(i, meta, order, slot, plane):
        return (lax.div(meta[0] + jnp.minimum(i * BATCH, jnp.maximum(meta[1] - 1, 0)), BATCH), 0)

    def whole(i, meta, order, slot, plane):
        return (0, 0, 0)

    row_spec = pl.BlockSpec((BATCH, vis_count), by_batch)
    hbm = pl.BlockSpec(memory_space=pl.ANY)
    operands = [tiles, observed, u, v, weight, *tables]
    in_specs = [hbm, hbm, row_spec, row_spec, row_spec] + [
        pl.BlockSpec(table.shape, whole) for table in tables
    ]
    aliases = {}
    if old is not None:
        operands.append(old)
        in_specs.append(hbm)
        aliases = {len(operands) + 3: 0}
    tile_shape, vis_shape = tiles.shape[1:], observed.shape[1:]
    return pl.pallas_call(
        functools.partial(block_kernel, aliased=old is not None),
        out_shape=(
            jax.ShapeDtypeStruct(observed.shape, jnp.float32),
            jax.ShapeDtypeStruct(tiles.shape, jnp.bfloat16),
        ),
        grid_spec=pltpu.PrefetchScalarGridSpec(
            num_scalar_prefetch=4,
            grid=((most + BATCH - 1) // BATCH,),
            in_specs=in_specs,
            out_specs=(hbm, hbm),
            scratch_shapes=[
                pltpu.VMEM((vis_count // TILE, BATCH * 2 * width, TILE), jnp.float32),
                pltpu.VMEM((width + 2, BATCH, vis_count), jnp.float32),
                pltpu.VMEM((2, BATCH) + tile_shape, jnp.bfloat16),
                pltpu.VMEM((2, BATCH) + vis_shape, jnp.float32),
                pltpu.VMEM((BATCH, 2 * width, 2 * pols * width), jnp.bfloat16),
                pltpu.VMEM((BATCH, 2 * width, 2 * pols * width), jnp.float32),
                pltpu.VMEM((BATCH,) + vis_shape, jnp.float32),
                pltpu.VMEM((BATCH,) + tile_shape, jnp.bfloat16),
                pltpu.SemaphoreType.DMA((2, 2, BATCH)),
                pltpu.SemaphoreType.DMA((2, BATCH)),
            ],
        ),
        input_output_aliases=aliases,
        compiler_params=pltpu.CompilerParams(vmem_limit_bytes=VMEM_BYTES),
        cost_estimate=pl.CostEstimate(
            flops=most * 2 * 2 * 2 * width * 2 * pols * width * vis_count,
            bytes_accessed=most * 2 * pols * vis_count * 40,
            transcendentals=0,
        ),
        name="process_blocks",
    )(meta, order, slot, plane, *operands)


def sum_kernel(requested, scale_ref, *refs, last):
    if last:
        old_ref, arrived_ref, out_ref = refs
        out_ref[...] = old_ref[...]
    else:
        arrived_ref, out_ref = refs
        out_ref[...] = jnp.zeros_like(out_ref)

    @pl.loop(0, arrived_ref.shape[0])
    def _(i):
        tile = requested[i]

        @pl.when(tile >= 0)
        def _():
            out_ref[tile] += arrived_ref[i].astype(jnp.float32)

    if last:
        out_ref[...] = out_ref[...] * scale_ref[0]


def sum_tiles(requested, scale, arrived, owned, old=None):
    shape = (owned,) + arrived.shape[1:]
    operands = [arrived] if old is None else [old, arrived]
    vmem = pl.BlockSpec(memory_space=pltpu.VMEM)
    return pl.pallas_call(
        functools.partial(sum_kernel, last=old is not None),
        out_shape=jax.ShapeDtypeStruct(shape, jnp.float32),
        in_specs=[pl.BlockSpec(memory_space=pltpu.SMEM)] * 2 + [vmem] * len(operands),
        out_specs=vmem,
        compiler_params=pltpu.CompilerParams(vmem_limit_bytes=VMEM_BYTES),
        cost_estimate=pl.CostEstimate(flops=arrived.size, bytes_accessed=arrived.size * 4, transcendentals=0),
        name="sum_tiles",
    )(requested, scale, *operands)


def kernel_tables(w_kernels, pols):
    planes, _, width, _ = w_kernels.shape
    half = width // 2
    real, imag = w_kernels[:, 0], w_kernels[:, 1]

    def offsets(table):
        return jnp.concatenate([table[:, half:], table[:, :1], table[:, half - 1 : 0 : -1]], axis=1)

    real_rows, imag_rows = offsets(real), offsets(imag)
    left = jnp.concatenate(
        [jnp.concatenate([real_rows, -imag_rows], axis=2), jnp.concatenate([imag_rows, real_rows], axis=2)], axis=1
    )
    back = jnp.swapaxes(left, 1, 2)
    real_columns, imag_columns = jnp.swapaxes(real_rows, 1, 2), jnp.swapaxes(imag_rows, 1, 2)
    right = jnp.concatenate(
        [
            jnp.stack([real_columns, imag_columns], axis=3),
            jnp.stack([-imag_columns, real_columns], axis=3),
        ],
        axis=1,
    )
    columns = jnp.swapaxes(right.reshape(planes, 2 * width, 2 * width), 1, 2).reshape(planes, 2 * width, 1, 2, 1, width)
    same = jnp.eye(pols, dtype=jnp.bool_).reshape(1, 1, pols, 1, pols, 1)
    turned = jnp.where(same, columns, jnp.zeros((), columns.dtype))
    turned = turned.reshape(planes, 2 * width * pols, 2 * width * pols)
    right = jnp.broadcast_to(right[..., None], right.shape + (pols,)).reshape(planes, 2 * width, 2 * width * pols)
    return left, back, right, turned


def exchange(operand):
    return lax.all_to_all(operand, AXES, split_axis=0, concat_axis=0, tiled=True)


def shards(vis_obs, uv_coords, vis_weight, block_group, tile_slot, w_plane, model_tiles, w_kernels):
    blocks = vis_obs.shape[0]
    pols = vis_obs.shape[2]
    groups = lax.axis_size(AXES)
    owned = model_tiles.shape[0]
    tile_shape = model_tiles.shape[1:]
    capacity = max(2, 2 * blocks // groups)
    early = max(1, 3 * capacity // 8)
    target = block_group[:, 0]
    markers = target[:, None] == jnp.arange(groups, dtype=jnp.int32)[None, :]
    counts = markers.astype(jnp.int32)
    before = jnp.cumsum(counts, axis=0) - counts
    rank = jnp.sum(jnp.where(markers, before, 0), axis=1)
    ranks = rank[:, None] == jnp.arange(capacity, dtype=jnp.int32)[None, :]
    wanted = jnp.sum(
        jnp.where(markers[:, :, None] & ranks[:, None, :], (tile_slot + 1)[:, None, None], 0), axis=0
    )
    own_weight = jnp.broadcast_to(jnp.sum(vis_weight)[None, None], (groups, 1))
    answers = exchange(jnp.concatenate([wanted.astype(jnp.float32), own_weight], axis=1))
    requested = answers[:, :capacity].astype(jnp.int32) - 1
    weight_sum = jnp.sum(answers[:, capacity])
    scaling = blocks * groups * vis_obs.shape[-1] / weight_sum
    scaling = scaling.reshape(1)

    tables = kernel_tables(w_kernels, pols)
    is_late = rank >= early
    late = is_late.astype(jnp.int32)
    early_count = blocks - jnp.sum(late)
    late_base = (early_count + BATCH - 1) // BATCH * BATCH
    item = jnp.where(is_late, late_base + jnp.cumsum(late) - 1, jnp.cumsum(1 - late) - 1)
    items = jnp.arange(blocks + BATCH, dtype=jnp.int32)
    order = jnp.sum(
        jnp.where(items[:, None] == item[None, :], jnp.arange(blocks, dtype=jnp.int32)[None, :], 0), axis=1
    )
    slot = jnp.where(is_late, target * (capacity - early) + rank - early, target * early + rank)
    u = jnp.take(uv_coords[:, 0], order, axis=0, mode="clip")
    v = jnp.take(uv_coords[:, 1], order, axis=0, mode="clip")
    weight = jnp.take(vis_weight, order, axis=0, mode="clip")

    def choose(part):
        chosen = jnp.take(model_tiles, jnp.maximum(part, 0).reshape(-1), axis=0, mode="clip")
        return chosen.reshape(part.shape + tile_shape)

    def send_tiles(chosen):
        return exchange(chosen).reshape((-1,) + tile_shape)

    def send_back(part):
        returned = exchange(part.reshape((groups, -1) + tile_shape))
        return returned.reshape(-1, tile_shape[0] * tile_shape[1], tile_shape[2])

    first, second = requested[:, :early], requested[:, early:]
    tiles_first = send_tiles(choose(first))
    chosen, order, slot, u, v, weight, tables = lax.optimization_barrier(
        (choose(second), order, slot, u, v, weight, tables)
    )
    tiles_second = send_tiles(chosen)
    given = (vis_obs, u, v, weight, tables)
    zero = jnp.zeros((), jnp.int32)
    residual, sent_first = process_blocks(
        blocks, zero, early_count, order, slot, w_plane, tiles_first, *given
    )
    late_most = blocks * (capacity - early) // capacity
    residual, sent_second = process_blocks(
        late_most, late_base, blocks - early_count, order, slot, w_plane, tiles_second, *given, residual
    )
    summed = sum_tiles(first.reshape(-1), scaling, send_back(sent_first), owned)
    summed = sum_tiles(second.reshape(-1), scaling, send_back(sent_second), owned, summed)
    return residual, summed.reshape(model_tiles.shape)


def solution(mesh):
    rows = P(AXES)
    in_specs = (rows,) * 7 + (P(),)
    return jax.shard_map(shards, mesh=mesh, in_specs=in_specs, out_specs=(rows, rows), check_vma=False)
```

```python
import functools
import math

import jax
import jax.numpy as jnp
import numpy as np
from jax import lax
from jax.experimental import pallas as pl
from jax.experimental.pallas import tpu as pltpu
from jax.sharding import Mesh
from jax.sharding import PartitionSpec as P

BATCH = 8
LANES = 512
TILE = 128
UNROLL = 4
VMEM_BYTES = 60 * 1024 * 1024
SIN_TERMS = [(-1.0) ** i * (2.0 * math.pi) ** (2 * i + 1) / math.factorial(2 * i + 1) for i in range(8)]
COS_TERMS = [(-1.0) ** i * (2.0 * math.pi) ** (2 * i) / math.factorial(2 * i) for i in range(9)]


def polynomial(terms, square):
    total = jnp.full_like(square, terms[-1])
    for term in terms[-2::-1]:
        total = total * square + term
    return total


def unit_phasor(turns):
    halves = jnp.floor(turns * 2.0 + 0.5)
    part = turns - halves * 0.5
    odd = halves - 2.0 * jnp.floor(halves * 0.5)
    sign = 1.0 - 2.0 * odd
    square = part * part
    return sign * polynomial(COS_TERMS, square), -sign * part * polynomial(SIN_TERMS, square)


def phasor_powers(cosine, sine, count):
    powers = {1: (cosine, sine)}
    for j in range(2, count + 1):
        ar, ai = powers[j // 2]
        br, bi = powers[j - j // 2]
        if j % 2 == 0:
            powers[j] = (ar * ar - ai * ai, 2.0 * ar * ai)
        else:
            powers[j] = (ar * br - ai * bi, ar * bi + ai * br)
    return powers


def rows_dot(left, right, left_dim, right_dim):
    return lax.dot_general(
        left, right, (((left_dim,), (right_dim,)), ((), ())), preferred_element_type=jnp.float32
    )


def split(value):
    high = value.astype(jnp.bfloat16)
    return high, (value - high.astype(jnp.float32)).astype(jnp.bfloat16)


def block_kernel(
    meta, order, slot, plane, tiles, observed, u_ref, v_ref, w_ref, left_ref, back_ref, right_ref, turned_ref, *rest, carried
):
    res, con, fu_ref, fv_ref, tile_buf, obs_buf, model_buf, grid_buf, res_buf, con_buf, in_sems, out_sems = rest[carried:]
    half = fv_ref.shape[0] // 2 - 1
    width = 2 * half
    pols = obs_buf.shape[3]
    span = pols * width
    vis_count = u_ref.shape[1]
    step = pl.program_id(0)
    base, count = meta[0], meta[1]

    def block_at(at, k):
        return order[base + jnp.minimum(at * BATCH + k, count - 1)]

    def incoming(at, k):
        block = block_at(at, k)
        turn = lax.rem(at, 2)
        return (
            pltpu.make_async_copy(tiles.at[slot[block]], tile_buf.at[turn, k], in_sems.at[0, turn, k]),
            pltpu.make_async_copy(observed.at[block], obs_buf.at[turn, k], in_sems.at[1, turn, k]),
        )

    def outgoing(at, k):
        block = block_at(at, k)
        return (
            pltpu.make_async_copy(con_buf.at[k], con.at[slot[block]], out_sems.at[0, k]),
            pltpu.make_async_copy(res_buf.at[k], res.at[block], out_sems.at[1, k]),
        )

    def start_incoming(at):
        for k in range(BATCH):
            for copy in incoming(at, k):
                copy.start()

    def make_phasors():
        cosine, sine = unit_phasor(u_ref[...] * (1.0 / width))
        powers = phasor_powers(cosine, sine, half)

        def put(row, value):
            for t in range(vis_count // TILE):
                fu_ref[t, row * BATCH : (row + 1) * BATCH, :] = value[:, t * TILE : (t + 1) * TILE]

        put(0, jnp.ones_like(cosine))
        put(width, jnp.zeros_like(cosine))
        for j in range(1, half + 1):
            real, imag = powers[j]
            if j < half:
                put(j, real)
                put(width + j, imag)
            low = half if j == half else half + j
            put(low, real)
            put(width + low, -imag)
        cosine, sine = unit_phasor(v_ref[...] * (1.0 / width))
        powers = phasor_powers(cosine, sine, half)
        for j in range(1, half + 1):
            fv_ref[j], fv_ref[half + 1 + j] = powers[j]

    wide = 2 * span
    unpaired = lax.broadcasted_iota(jnp.int32, (2 * width, span), 1) < 2 * pols

    def paired(full):
        first, second = full[:, :span], full[:, span:]
        total = jnp.where(unpaired, first, first + second)
        change = jnp.where(unpaired, second, first - second)
        return jnp.concatenate([total, change], axis=1)

    def from_right(which):
        band = lax.rem(lax.broadcasted_iota(jnp.int32, (width, wide), 1), pols)
        table = right_ref[which]
        zero = jnp.zeros((), jnp.bfloat16)
        return jnp.concatenate(
            [jnp.where(band == p, table[r * width : (r + 1) * width], zero) for r in range(2) for p in range(pols)],
            axis=0,
        )

    def make_model(k):
        which = plane[block_at(step, k)]
        tile = tile_buf[lax.rem(step, 2), k].reshape(2 * width, span)
        left = rows_dot(left_ref[which], tile, 1, 0).astype(jnp.bfloat16)
        left_real, left_imag = left[:width], left[width:]
        left = jnp.concatenate(
            [jnp.concatenate([left_real, left_imag], axis=1), jnp.concatenate([-left_imag, left_real], axis=1)],
            axis=0,
        )
        model_buf[k] = paired(rows_dot(left, from_right(which), 1, 0)).astype(jnp.bfloat16)

    turn = jnp.where(lax.broadcasted_iota(jnp.int32, (2 * pols, LANES), 0) < pols, -1.0, 1.0)

    def degrid_and_grid(k):
        model = model_buf[k]
        gridded = None
        for start in range(0, vis_count, LANES):
            lanes = pl.ds(start, LANES)
            along_u = jnp.concatenate(
                [
                    fu_ref[start // TILE + t, pl.ds(k, 2 * width, stride=BATCH), :]
                    for t in range(LANES // TILE)
                ],
                axis=1,
            ).astype(jnp.bfloat16)
            spread = rows_dot(model, along_u, 0, 0).reshape(width, 2 * pols, LANES)

            def phase(index):
                return jnp.broadcast_to(fv_ref[index, pl.ds(k, 1), lanes], (2 * pols, LANES))

            cos_part = spread[0] + spread[half] * phase(half)
            sin_part = -spread[half] * phase(2 * half + 1)
            for j in range(1, half):
                cos_part = cos_part + spread[j] * phase(j)
                sin_part = sin_part + spread[half + j] * phase(half + 1 + j)
            predicted = cos_part + turn * jnp.roll(sin_part, pols, axis=0)
            given = obs_buf[lax.rem(step, 2), k, :, :, lanes]
            residual = jnp.concatenate([given[0], given[1]], axis=0) - predicted * (1.0 / width)
            res_buf[k, 0, :, lanes] = residual[:pols]
            res_buf[k, 1, :, lanes] = residual[pols:]
            scaled = residual * (w_ref[pl.ds(k, 1), lanes] * (1.0 / width))
            turned = -turn * jnp.roll(scaled, pols, axis=0)
            cos_rows, sin_rows = [scaled], [scaled * phase(half) - turned * phase(2 * half + 1)]
            for j in range(1, half):
                cos_rows.append(scaled * phase(j))
                sin_rows.append(turned * phase(half + 1 + j))
            weighted = jnp.concatenate(cos_rows + sin_rows, axis=0).astype(jnp.bfloat16)
            part = rows_dot(along_u, weighted, 1, 1)
            gridded = part if gridded is None else gridded + part
        grid_buf[k] = gridded

    def make_contribution(k):
        which = plane[block_at(step, k)]
        back = rows_dot(jnp.concatenate(split(paired(grid_buf[k])), axis=0), turned_ref[which], 1, 0)
        back = back[: 2 * width] + back[2 * width :]
        back_real = back[:width, :span] + back[width:, span:]
        back_imag = back[:width, span:] - back[width:, :span]
        back = jnp.concatenate([back_real, back_imag], axis=0)
        result = rows_dot(back_ref[which], jnp.concatenate(split(back), axis=1), 1, 0)
        result = result[:, :span] + result[:, span:]
        con_buf[k] = result.astype(con_buf.dtype).reshape(con_buf.shape[1:])

    @pl.when(step * BATCH < count)
    def _():
        @pl.when(step == 0)
        def _():
            start_incoming(step)

        @pl.when((step + 1) * BATCH < count)
        def _():
            start_incoming(step + 1)

        make_phasors()
        for k in range(BATCH):
            for copy in incoming(step, k):
                copy.wait()
        for k in range(BATCH):
            make_model(k)

        @pl.when(step > 0)
        def _():
            for k in range(BATCH):
                for copy in outgoing(step - 1, k):
                    copy.wait()

        @pl.loop(0, BATCH // UNROLL)
        def _(i):
            for k in range(UNROLL):
                degrid_and_grid(i * UNROLL + k)

        for k in range(BATCH):
            make_contribution(k)
        last = (step + 1) * BATCH >= count
        for k in range(BATCH):

            @pl.when(step * BATCH + k < count)
            def _():
                for copy in outgoing(step, k):
                    copy.start()

        for k in range(BATCH):

            @pl.when(last & (step * BATCH + k < count))
            def _():
                for copy in outgoing(step, k):
                    copy.wait()


def process_blocks(most, base, count, order, slot, plane, tiles, observed, u, v, weight, tables, carried=()):
    pols, vis_count = observed.shape[2:]
    width = tiles.shape[2]
    meta = jnp.stack([base, count]).astype(jnp.int32)

    def by_batch(i, meta, order, slot, plane):
        return (lax.div(meta[0] + jnp.minimum(i * BATCH, jnp.maximum(meta[1] - 1, 0)), BATCH), 0)

    def whole(i, meta, order, slot, plane):
        return (0, 0, 0)

    row_spec = pl.BlockSpec((BATCH, vis_count), by_batch)
    hbm = pl.BlockSpec(memory_space=pl.ANY)
    operands = [tiles, observed, u, v, weight, *tables]
    in_specs = [hbm, hbm, row_spec, row_spec, row_spec] + [
        pl.BlockSpec(table.shape, whole) for table in tables
    ]
    aliases = {len(operands) + 4 + i: i for i in range(len(carried))}
    operands += carried
    in_specs += [hbm] * len(carried)
    tile_shape, vis_shape = tiles.shape[1:], observed.shape[1:]
    return pl.pallas_call(
        functools.partial(block_kernel, carried=len(carried)),
        out_shape=(
            jax.ShapeDtypeStruct(observed.shape, jnp.float32),
            jax.ShapeDtypeStruct(tiles.shape, jnp.bfloat16),
        ),
        grid_spec=pltpu.PrefetchScalarGridSpec(
            num_scalar_prefetch=4,
            grid=((most + BATCH - 1) // BATCH,),
            in_specs=in_specs,
            out_specs=(hbm, hbm),
            scratch_shapes=[
                pltpu.VMEM((vis_count // TILE, BATCH * 2 * width, TILE), jnp.float32),
                pltpu.VMEM((width + 2, BATCH, vis_count), jnp.float32),
                pltpu.VMEM((2, BATCH) + tile_shape, jnp.bfloat16),
                pltpu.VMEM((2, BATCH) + vis_shape, jnp.float32),
                pltpu.VMEM((BATCH, 2 * width, 2 * pols * width), jnp.bfloat16),
                pltpu.VMEM((BATCH, 2 * width, 2 * pols * width), jnp.float32),
                pltpu.VMEM((BATCH,) + vis_shape, jnp.float32),
                pltpu.VMEM((BATCH,) + tile_shape, jnp.bfloat16),
                pltpu.SemaphoreType.DMA((2, 2, BATCH)),
                pltpu.SemaphoreType.DMA((2, BATCH)),
            ],
        ),
        input_output_aliases=aliases,
        compiler_params=pltpu.CompilerParams(vmem_limit_bytes=VMEM_BYTES),
        cost_estimate=pl.CostEstimate(
            flops=most * 2 * 2 * 2 * width * 2 * pols * width * vis_count,
            bytes_accessed=most * 2 * pols * vis_count * 40,
            transcendentals=0,
        ),
        name="process_blocks",
    )(meta, order, slot, plane, *operands)


def sum_kernel(requested, arrived_ref, out_ref, total_ref):
    total_ref[...] = jnp.zeros_like(total_ref)

    @pl.loop(0, arrived_ref.shape[0])
    def _(i):
        tile = requested[i]

        @pl.when(tile >= 0)
        def _():
            total_ref[tile] += arrived_ref[i].astype(jnp.float32)

    out_ref[...] = total_ref[...].astype(out_ref.dtype)


def sum_tiles(requested, arrived, owned, dtype):
    shape = (owned,) + arrived.shape[1:]
    vmem = pl.BlockSpec(memory_space=pltpu.VMEM)
    return pl.pallas_call(
        sum_kernel,
        out_shape=jax.ShapeDtypeStruct(shape, dtype),
        in_specs=[pl.BlockSpec(memory_space=pltpu.SMEM), vmem],
        out_specs=vmem,
        scratch_shapes=[pltpu.VMEM(shape, jnp.float32)],
        compiler_params=pltpu.CompilerParams(vmem_limit_bytes=VMEM_BYTES),
        cost_estimate=pl.CostEstimate(flops=arrived.size, bytes_accessed=arrived.size * 4, transcendentals=0),
        name="sum_tiles",
    )(requested, arrived)


def table_kernel(planes_ref, signs_ref, spread_ref, gather_ref, repeat_ref, left_ref, back_ref, right_ref, turned_ref):
    size = left_ref.shape[1]
    wide = right_ref.shape[2]
    pols = wide // size
    row = lax.rem(lax.broadcasted_iota(jnp.int32, (wide, wide), 0), pols)
    column = lax.rem(lax.div(lax.broadcasted_iota(jnp.int32, (wide, wide), 1), size // 2), pols)
    same = row == column
    zero = jnp.zeros((), jnp.bfloat16)

    def exact(left, right, left_dim=1):
        return rows_dot(left, right, left_dim, 0).astype(jnp.bfloat16)

    for k in range(planes_ref.shape[0]):
        both = exact(signs_ref[...], planes_ref[k])
        left = jnp.concatenate([both[:size], both[size:]], axis=1)
        left_ref[k] = left
        back = exact(left, jnp.eye(size, dtype=jnp.bfloat16), 0)
        back_ref[k] = back
        right_ref[k] = exact(back, spread_ref[...])
        turned_ref[k] = jnp.where(same, exact(exact(gather_ref[...], left), repeat_ref[...]), zero)


def kernel_tables(w_kernels, pols):
    planes, _, width, _ = w_kernels.shape
    half = width // 2
    size, wide = 2 * width, 2 * width * pols
    rows = np.concatenate([np.arange(half, width), [0], np.arange(half - 1, 0, -1)])
    pick = np.eye(width)[rows]
    none = np.zeros_like(pick)
    signs = np.block([[pick, none], [none, pick], [none, -pick], [pick, none]])
    spread = np.zeros((2, width, width, 2, pols))
    repeat = np.zeros((2, width, 2, pols, width))
    for r in range(2):
        for n in range(width):
            spread[r, n, n, r] = 1.0
            repeat[r, n, r, :, n] = 1.0
    spread, repeat = spread.reshape(size, wide), repeat.reshape(size, wide)
    constants = [jnp.asarray(table, jnp.bfloat16) for table in (signs, spread, spread.T, repeat)]
    part = math.gcd(planes, 8)

    def by_part(shape):
        return pl.BlockSpec((part,) + shape, lambda i: (i, 0, 0))

    shapes = [(size, size), (size, size), (size, wide), (wide, wide)]
    return pl.pallas_call(
        table_kernel,
        grid=(planes // part,),
        out_shape=[jax.ShapeDtypeStruct((planes,) + shape, jnp.bfloat16) for shape in shapes],
        in_specs=[by_part((size, width))] + [pl.BlockSpec(table.shape, lambda i: (0, 0)) for table in constants],
        out_specs=[by_part(shape) for shape in shapes],
        compiler_params=pltpu.CompilerParams(vmem_limit_bytes=VMEM_BYTES),
        name="kernel_tables",
    )(w_kernels.reshape(planes, size, width), *constants)


def shards(vis_obs, uv_coords, vis_weight, block_group, tile_slot, w_plane, model_tiles, w_kernels):
    blocks, _, pols, vis_count = vis_obs.shape
    peers = lax.axis_size("peer")
    groups = 2 * peers
    owned = model_tiles.shape[0]
    tile_shape = model_tiles.shape[1:]
    flat_shape = (tile_shape[0] * tile_shape[1], tile_shape[2])
    capacity = max(2, 2 * blocks // groups)
    swap = [(0, 1), (1, 0)]
    mirrored = lax.ppermute(model_tiles, "half", swap)

    target = block_group[:, 0]
    far = lax.rem(lax.div(target, peers) + lax.axis_index("half"), 2)
    peer = lax.rem(target, peers)
    holder = far * peers + peer
    markers = holder[:, None] == jnp.arange(groups, dtype=jnp.int32)[None, :]
    counts = markers.astype(jnp.int32)
    before = jnp.cumsum(counts, axis=0) - counts
    rank = jnp.sum(jnp.where(markers, before, 0), axis=1)
    ranks = rank[:, None] == jnp.arange(capacity, dtype=jnp.int32)[None, :]
    wanted = jnp.sum(
        jnp.where(markers[:, :, None] & ranks[:, None, :], (tile_slot + 1)[:, None, None], 0), axis=0
    ).astype(jnp.float32)
    own_weight = jnp.broadcast_to(jnp.sum(vis_weight)[None, None], (peers, 1))

    def exchange(operand):
        return lax.all_to_all(operand, "peer", split_axis=0, concat_axis=0, tiled=True)

    answers = exchange(jnp.concatenate([wanted[:peers], wanted[peers:], own_weight], axis=1))
    near_request = answers[:, :capacity].astype(jnp.int32) - 1
    far_request = answers[:, capacity : 2 * capacity].astype(jnp.int32) - 1
    half_weight = jnp.sum(answers[:, 2 * capacity]).reshape(1)
    weight_sum = half_weight + lax.ppermute(half_weight, "half", swap)
    scaling = blocks * groups * vis_count / weight_sum

    tables = kernel_tables(w_kernels, pols)
    near_count = blocks - jnp.sum(far)
    far_base = (near_count + BATCH - 1) // BATCH * BATCH
    item = jnp.where(far == 1, far_base + jnp.cumsum(far) - 1, jnp.cumsum(1 - far) - 1)
    items = jnp.arange(blocks + BATCH, dtype=jnp.int32)
    order = jnp.sum(
        jnp.where(items[:, None] == item[None, :], jnp.arange(blocks, dtype=jnp.int32)[None, :], 0), axis=1
    )
    slot = peer * capacity + rank
    u = jnp.take(uv_coords[:, 0], order, axis=0, mode="clip")
    v = jnp.take(uv_coords[:, 1], order, axis=0, mode="clip")
    weight = jnp.take(vis_weight, order, axis=0, mode="clip")

    def choose(tiles, request):
        chosen = jnp.take(tiles, jnp.maximum(request, 0).reshape(-1), axis=0, mode="clip")
        return chosen.reshape(request.shape + tile_shape)

    def send_tiles(chosen):
        return exchange(chosen).reshape((-1,) + tile_shape)

    def send_back(part, request, dtype):
        returned = exchange(part.reshape((peers, capacity) + tile_shape)).reshape((-1,) + flat_shape)
        return sum_tiles(request.reshape(-1), returned, owned, dtype)

    near_tiles = send_tiles(choose(model_tiles, near_request))
    chosen, order, slot, u, v, weight, tables = lax.optimization_barrier(
        (choose(mirrored, far_request), order, slot, u, v, weight, tables)
    )
    far_tiles = send_tiles(chosen)
    given = (vis_obs, u, v, weight, tables)
    zero = jnp.zeros((), jnp.int32)
    opening = max(BATCH, blocks // 4 // BATCH * BATCH)
    first_count = jnp.minimum(near_count, opening)
    residual, near_sent = process_blocks(opening, zero, first_count, order, slot, w_plane, near_tiles, *given)
    residual, far_sent = process_blocks(
        blocks, far_base, blocks - near_count, order, slot, w_plane, far_tiles, *given, (residual,)
    )
    relayed = lax.ppermute(send_back(far_sent, far_request, jnp.bfloat16), "half", swap)
    residual, near_sent = process_blocks(
        blocks - opening,
        zero + opening,
        near_count - first_count,
        order,
        slot,
        w_plane,
        near_tiles,
        *given,
        (residual, near_sent),
    )
    summed = send_back(near_sent, near_request, jnp.float32)
    summed = (summed + relayed.astype(jnp.float32)) * scaling
    return residual, summed.reshape(model_tiles.shape)


def solution(mesh):
    devices = mesh.devices.reshape(2, -1)
    halves = Mesh(devices, ("half", "peer"))
    rows = P(("half", "peer"))
    in_specs = (rows,) * 7 + (P(),)
    return jax.shard_map(shards, mesh=halves, in_specs=in_specs, out_specs=(rows, rows), check_vma=False)
```

```python
import functools
import math

import jax
import jax.numpy as jnp
import numpy as np
from jax import lax
from jax.experimental import pallas as pl
from jax.experimental.pallas import tpu as pltpu
from jax.sharding import Mesh
from jax.sharding import PartitionSpec as P

BATCH = 8
LANES = 512
TILE = 128
ROWS = 8
UNROLL = 8
VMEM_BYTES = 60 * 1024 * 1024
SIN_TERMS = [(-1.0) ** i * (2.0 * math.pi) ** (2 * i + 1) / math.factorial(2 * i + 1) for i in range(8)]
COS_TERMS = [(-1.0) ** i * (2.0 * math.pi) ** (2 * i) / math.factorial(2 * i) for i in range(9)]


def polynomial(terms, square):
    total = jnp.full_like(square, terms[-1])
    for term in terms[-2::-1]:
        total = total * square + term
    return total


def unit_phasor(turns):
    halves = jnp.floor(turns * 2.0 + 0.5)
    part = turns - halves * 0.5
    odd = halves - 2.0 * jnp.floor(halves * 0.5)
    sign = 1.0 - 2.0 * odd
    square = part * part
    return sign * polynomial(COS_TERMS, square), -sign * part * polynomial(SIN_TERMS, square)


def phasor_powers(cosine, sine, count):
    powers = {1: (cosine, sine)}
    for j in range(2, count + 1):
        ar, ai = powers[j // 2]
        br, bi = powers[j - j // 2]
        if j % 2 == 0:
            powers[j] = (ar * ar - ai * ai, 2.0 * ar * ai)
        else:
            powers[j] = (ar * br - ai * bi, ar * bi + ai * br)
    return powers


def rows_dot(left, right, left_dim, right_dim):
    return lax.dot_general(
        left, right, (((left_dim,), (right_dim,)), ((), ())), preferred_element_type=jnp.float32
    )


def split(value):
    high = value.astype(jnp.bfloat16)
    return high, (value - high.astype(jnp.float32)).astype(jnp.bfloat16)


def block_kernel(
    meta, order, slot, plane, tiles, observed, u_ref, v_ref, w_ref, left_ref, back_ref, right_ref, turned_ref, *rest, carried
):
    res, con, fu_ref, fv_ref, tile_buf, obs_buf, model_buf, grid_buf, res_buf, con_buf, in_sems, out_sems = rest[carried:]
    quarter = fv_ref.shape[0] // 2 - 1
    half = 2 * quarter
    width = 2 * half
    pols = obs_buf.shape[3]
    span = pols * width
    vis_count = u_ref.shape[1]
    step = pl.program_id(0)
    base, count = meta[0], meta[1]

    def block_at(at, k):
        return order[base + jnp.minimum(at * BATCH + k, count - 1)]

    def incoming(at, k):
        block = block_at(at, k)
        turn = lax.rem(at, 2)
        return (
            pltpu.make_async_copy(tiles.at[slot[block]], tile_buf.at[turn, k], in_sems.at[0, turn, k]),
            pltpu.make_async_copy(observed.at[block], obs_buf.at[turn, k], in_sems.at[1, turn, k]),
        )

    def outgoing(at, k):
        block = block_at(at, k)
        return (
            pltpu.make_async_copy(con_buf.at[k], con.at[slot[block]], out_sems.at[0, k]),
            pltpu.make_async_copy(res_buf.at[k], res.at[block], out_sems.at[1, k]),
        )

    def start_incoming(at):
        for k in range(BATCH):
            for copy in incoming(at, k):
                copy.start()

    def make_phasors():
        cosine, sine = unit_phasor(u_ref[...] * (1.0 / width))
        powers = phasor_powers(cosine, sine, half)

        def put(row, value):
            for t in range(vis_count // TILE):
                fu_ref[t, row * BATCH : (row + 1) * BATCH, :] = value[:, t * TILE : (t + 1) * TILE]

        put(0, jnp.ones_like(cosine))
        put(half, powers[half][0])
        put(width, powers[half][1])
        for j in range(1, half):
            real, imag = powers[j]
            put(j, real)
            put(half + j, imag)
        for j in range(1, ROWS):
            put(width + j, jnp.zeros_like(cosine))
        cosine, sine = unit_phasor(v_ref[...] * (1.0 / width))
        powers = phasor_powers(cosine, sine, quarter)
        for j in range(1, quarter + 1):
            fv_ref[j], fv_ref[quarter + 1 + j] = powers[j]

    wide = 2 * span
    basis = 2 * (width + ROWS)
    lane = lax.broadcasted_iota(jnp.int32, (basis, span), 1)
    unpaired = lax.rem(lane, span // 2) < 2 * pols
    direct = lane < span // 2
    start_row = lax.broadcasted_iota(jnp.int32, (half, span), 0) == 0
    lone_row = start_row[:ROWS]

    def paired(full):
        other = jnp.roll(full, span // 2, axis=1)
        return jnp.where(unpaired, full, jnp.where(direct, full + other, other - full))

    def fold(full):
        total, change = full[:, :span] + full[:, span:], full[:, :span] - full[:, span:]

        def pairs(real, imag):
            ahead, behind = real[:half], real[half:]
            above, below = imag[:half], imag[half:]
            return [jnp.where(start_row, ahead, ahead + behind), jnp.where(start_row, behind, above - below)], (
                jnp.where(lone_row, -below[:ROWS], 0.0)
            )

        cos_pairs, cos_lone = pairs(total[:width], total[width:])
        sin_pairs, sin_lone = pairs(change[width:], -change[:width])
        return paired(jnp.concatenate(cos_pairs + sin_pairs + [cos_lone, sin_lone], axis=0))

    def unfold(sums):
        sums = paired(sums)
        cos_cos, sin_cos, cos_sin, sin_sin = [sums[i * half : (i + 1) * half] for i in range(4)]
        lone_cos = sums[4 * half :]
        lone_sin = jnp.concatenate([sums[4 * half + ROWS :]] * 2, axis=0)
        ahead = [cos_cos, jnp.where(start_row, 0.0, sin_cos), cos_sin, jnp.where(start_row, 0.0, sin_sin)]
        behind = [
            jnp.where(start_row, sin_cos, cos_cos),
            -jnp.where(start_row, lone_cos, sin_cos),
            jnp.where(start_row, sin_sin, cos_sin),
            -jnp.where(start_row, lone_sin, sin_sin),
        ]
        columns = []
        for side in (1.0, -1.0):
            rows = [[cc - side * ss, sc + side * cs] for cc, sc, cs, ss in (ahead, behind)]
            columns.append(jnp.concatenate([rows[0][0], rows[1][0], rows[0][1], rows[1][1]], axis=0))
        return jnp.concatenate(columns, axis=1)

    def from_right(which):
        band = lax.rem(lax.broadcasted_iota(jnp.int32, (width, wide), 1), pols)
        table = right_ref[which]
        zero = jnp.zeros((), jnp.bfloat16)
        return jnp.concatenate(
            [jnp.where(band == p, table[r * width : (r + 1) * width], zero) for r in range(2) for p in range(pols)],
            axis=0,
        )

    def make_model(k):
        which = plane[block_at(step, k)]
        tile = tile_buf[lax.rem(step, 2), k].reshape(2 * width, span)
        left = rows_dot(left_ref[which], tile, 1, 0).astype(jnp.bfloat16)
        left_real, left_imag = left[:width], left[width:]
        left = jnp.concatenate(
            [jnp.concatenate([left_real, left_imag], axis=1), jnp.concatenate([-left_imag, left_real], axis=1)],
            axis=0,
        )
        model_buf[k] = fold(rows_dot(left, from_right(which), 1, 0)).astype(jnp.bfloat16)

    turn = jnp.where(lax.broadcasted_iota(jnp.int32, (2 * pols, LANES), 0) < pols, -1.0, 1.0)

    def degrid_and_grid(k):
        model = model_buf[k]
        gridded = None
        for start in range(0, vis_count, LANES):
            lanes = pl.ds(start, LANES)
            along_u = jnp.concatenate(
                [
                    fu_ref[start // TILE + t, pl.ds(k, width + ROWS, stride=BATCH), :]
                    for t in range(LANES // TILE)
                ],
                axis=1,
            ).reshape((width + ROWS) // ROWS, ROWS, LANES)

            def phase(index):
                return jnp.broadcast_to(fv_ref[index, pl.ds(k, 1), lanes], (2 * pols, LANES))

            far_cos, far_sin = phase(quarter), phase(2 * quarter + 1)
            main, lone = along_u[: width // ROWS], along_u[width // ROWS :]
            along = jnp.concatenate([main * far_cos, main * far_sin, lone * far_cos, lone * far_sin], axis=0)
            along = along.reshape(basis, LANES).astype(jnp.bfloat16)
            spread = rows_dot(model, along, 0, 0).reshape(half, 2 * pols, LANES)
            cos_part = spread[0] + spread[quarter] * far_cos
            sin_part = -spread[quarter] * far_sin
            for j in range(1, quarter):
                cos_part = cos_part + spread[j] * phase(j)
                sin_part = sin_part + spread[quarter + j] * phase(quarter + 1 + j)
            predicted = cos_part + turn * jnp.roll(sin_part, pols, axis=0)
            given = obs_buf[lax.rem(step, 2), k, :, :, lanes]
            residual = jnp.concatenate([given[0], given[1]], axis=0) - predicted * (1.0 / width)
            res_buf[k, 0, :, lanes] = residual[:pols]
            res_buf[k, 1, :, lanes] = residual[pols:]
            scaled = residual * (w_ref[pl.ds(k, 1), lanes] * (1.0 / width))
            turned = -turn * jnp.roll(scaled, pols, axis=0)
            cos_rows, sin_rows = [scaled], [scaled * far_cos - turned * far_sin]
            for j in range(1, quarter):
                cos_rows.append(scaled * phase(j))
                sin_rows.append(turned * phase(quarter + 1 + j))
            weighted = jnp.concatenate(cos_rows + sin_rows, axis=0).astype(jnp.bfloat16)
            part = rows_dot(along, weighted, 1, 1)
            gridded = part if gridded is None else gridded + part
        grid_buf[k] = gridded

    def make_contribution(k):
        which = plane[block_at(step, k)]
        back = rows_dot(jnp.concatenate(split(unfold(grid_buf[k])), axis=0), turned_ref[which], 1, 0)
        back = back[: 2 * width] + back[2 * width :]
        back_real = back[:width, :span] + back[width:, span:]
        back_imag = back[:width, span:] - back[width:, :span]
        back = jnp.concatenate([back_real, back_imag], axis=0)
        result = rows_dot(back_ref[which], jnp.concatenate(split(back), axis=1), 1, 0)
        result = result[:, :span] + result[:, span:]
        con_buf[k] = result.astype(con_buf.dtype).reshape(con_buf.shape[1:])

    @pl.when(step * BATCH < count)
    def _():
        @pl.when(step == 0)
        def _():
            start_incoming(step)

        @pl.when((step + 1) * BATCH < count)
        def _():
            start_incoming(step + 1)

        make_phasors()
        for k in range(BATCH):
            for copy in incoming(step, k):
                copy.wait()
        for k in range(BATCH):
            make_model(k)

        @pl.when(step > 0)
        def _():
            for k in range(BATCH):
                for copy in outgoing(step - 1, k):
                    copy.wait()

        @pl.loop(0, BATCH // UNROLL)
        def _(i):
            for k in range(UNROLL):
                degrid_and_grid(i * UNROLL + k)

        for k in range(BATCH):
            make_contribution(k)
        last = (step + 1) * BATCH >= count
        for k in range(BATCH):

            @pl.when(step * BATCH + k < count)
            def _():
                for copy in outgoing(step, k):
                    copy.start()

        for k in range(BATCH):

            @pl.when(last & (step * BATCH + k < count))
            def _():
                for copy in outgoing(step, k):
                    copy.wait()


def process_blocks(most, base, count, order, slot, plane, tiles, observed, u, v, weight, tables, carried=()):
    pols, vis_count = observed.shape[2:]
    width = tiles.shape[2]
    meta = jnp.stack([base, count]).astype(jnp.int32)

    def by_batch(i, meta, order, slot, plane):
        return (lax.div(meta[0] + jnp.minimum(i * BATCH, jnp.maximum(meta[1] - 1, 0)), BATCH), 0)

    def whole(i, meta, order, slot, plane):
        return (0, 0, 0)

    row_spec = pl.BlockSpec((BATCH, vis_count), by_batch)
    hbm = pl.BlockSpec(memory_space=pl.ANY)
    operands = [tiles, observed, u, v, weight, *tables]
    in_specs = [hbm, hbm, row_spec, row_spec, row_spec] + [
        pl.BlockSpec(table.shape, whole) for table in tables
    ]
    aliases = {len(operands) + 4 + i: i for i in range(len(carried))}
    operands += carried
    in_specs += [hbm] * len(carried)
    tile_shape, vis_shape = tiles.shape[1:], observed.shape[1:]
    return pl.pallas_call(
        functools.partial(block_kernel, carried=len(carried)),
        out_shape=(
            jax.ShapeDtypeStruct(observed.shape, jnp.float32),
            jax.ShapeDtypeStruct(tiles.shape, jnp.bfloat16),
        ),
        grid_spec=pltpu.PrefetchScalarGridSpec(
            num_scalar_prefetch=4,
            grid=((most + BATCH - 1) // BATCH,),
            in_specs=in_specs,
            out_specs=(hbm, hbm),
            scratch_shapes=[
                pltpu.VMEM((vis_count // TILE, BATCH * (width + ROWS), TILE), jnp.float32),
                pltpu.VMEM((width // 2 + 2, BATCH, vis_count), jnp.float32),
                pltpu.VMEM((2, BATCH) + tile_shape, jnp.bfloat16),
                pltpu.VMEM((2, BATCH) + vis_shape, jnp.float32),
                pltpu.VMEM((BATCH, 2 * (width + ROWS), pols * width), jnp.bfloat16),
                pltpu.VMEM((BATCH, 2 * (width + ROWS), pols * width), jnp.float32),
                pltpu.VMEM((BATCH,) + vis_shape, jnp.float32),
                pltpu.VMEM((BATCH,) + tile_shape, jnp.bfloat16),
                pltpu.SemaphoreType.DMA((2, 2, BATCH)),
                pltpu.SemaphoreType.DMA((2, BATCH)),
            ],
        ),
        input_output_aliases=aliases,
        compiler_params=pltpu.CompilerParams(vmem_limit_bytes=VMEM_BYTES),
        cost_estimate=pl.CostEstimate(
            flops=most * 2 * 2 * 2 * width * 2 * pols * width * vis_count,
            bytes_accessed=most * 2 * pols * vis_count * 40,
            transcendentals=0,
        ),
        name="process_blocks",
    )(meta, order, slot, plane, *operands)


def sum_kernel(requested, *refs, carried):
    if carried:
        scale_ref, arrived_ref, *old_refs, out_ref, total_ref = refs
        start = 0
        for old_ref in old_refs:
            rows = old_ref.shape[1]
            total_ref[:, start : start + rows] = old_ref[...].astype(jnp.float32)
            start += rows
    else:
        arrived_ref, out_ref, total_ref = refs
        total_ref[...] = jnp.zeros_like(total_ref)

    @pl.loop(0, arrived_ref.shape[0])
    def _(i):
        tile = requested[i]

        @pl.when(tile >= 0)
        def _():
            total_ref[tile] += arrived_ref[i].astype(jnp.float32)

    total = total_ref[...] * scale_ref[0] if carried else total_ref[...]
    out_ref[...] = total.astype(out_ref.dtype)


def sum_tiles(requested, arrived, owned, dtype, scale=None, old=()):
    shape = (owned,) + arrived.shape[1:]
    vmem, smem = pl.BlockSpec(memory_space=pltpu.VMEM), pl.BlockSpec(memory_space=pltpu.SMEM)
    carried = len(old) > 0
    return pl.pallas_call(
        functools.partial(sum_kernel, carried=carried),
        out_shape=jax.ShapeDtypeStruct(shape, dtype),
        in_specs=[smem, smem, vmem] + [vmem] * len(old) if carried else [smem, vmem],
        out_specs=vmem,
        scratch_shapes=[pltpu.VMEM(shape, jnp.float32)],
        compiler_params=pltpu.CompilerParams(vmem_limit_bytes=VMEM_BYTES),
        cost_estimate=pl.CostEstimate(flops=arrived.size, bytes_accessed=arrived.size * 4, transcendentals=0),
        name="sum_tiles",
    )(requested, *((scale, arrived, *old) if carried else (arrived,)))


def table_kernel(planes_ref, signs_ref, columns_ref, spread_ref, gather_ref, repeat_ref, left_ref, back_ref, right_ref, turned_ref):
    size = left_ref.shape[1]
    wide = right_ref.shape[2]
    pols = wide // size
    row = lax.rem(lax.broadcasted_iota(jnp.int32, (wide, wide), 0), pols)
    column = lax.rem(lax.div(lax.broadcasted_iota(jnp.int32, (wide, wide), 1), size // 2), pols)
    same = row == column
    zero = jnp.zeros((), jnp.bfloat16)

    def exact(left, right, left_dim=1):
        return rows_dot(left, right, left_dim, 0).astype(jnp.bfloat16)

    for k in range(planes_ref.shape[0]):
        def embed(signs):
            both = exact(signs, planes_ref[k])
            return jnp.concatenate([both[:size], both[size:]], axis=1)

        left = embed(signs_ref[...])
        left_ref[k] = left
        back = exact(left, jnp.eye(size, dtype=jnp.bfloat16), 0)
        back_ref[k] = back
        columns = embed(columns_ref[...])
        right_ref[k] = exact(columns, spread_ref[...], 0)
        turned_ref[k] = jnp.where(same, exact(exact(gather_ref[...], columns), repeat_ref[...]), zero)


def kernel_tables(w_kernels, pols):
    planes, _, width, _ = w_kernels.shape
    half = width // 2
    size, wide = 2 * width, 2 * width * pols


    def signs(offsets):
        pick = np.eye(width)[np.array(offsets) + half]
        none = np.zeros_like(pick)
        return np.block([[pick, none], [none, pick], [none, -pick], [pick, none]])

    def paired(count):
        return [*range(count), -count, *range(-1, -count, -1)]

    quarter = half // 2
    rows = signs(paired(half))
    columns = signs([c + side * quarter for side in (1, -1) for c in paired(quarter)])
    spread = np.zeros((2, width, width, 2, pols))
    repeat = np.zeros((2, width, 2, pols, width))
    for r in range(2):
        for n in range(width):
            spread[r, n, n, r] = 1.0
            repeat[r, n, r, :, n] = 1.0
    spread, repeat = spread.reshape(size, wide), repeat.reshape(size, wide)
    constants = [jnp.asarray(table, jnp.bfloat16) for table in (rows, columns, spread, spread.T, repeat)]
    part = math.gcd(planes, 8)

    def by_part(shape):
        return pl.BlockSpec((part,) + shape, lambda i: (i, 0, 0))

    shapes = [(size, size), (size, size), (size, wide), (wide, wide)]
    return pl.pallas_call(
        table_kernel,
        grid=(planes // part,),
        out_shape=[jax.ShapeDtypeStruct((planes,) + shape, jnp.bfloat16) for shape in shapes],
        in_specs=[by_part((size, width))] + [pl.BlockSpec(table.shape, lambda i: (0, 0)) for table in constants],
        out_specs=[by_part(shape) for shape in shapes],
        compiler_params=pltpu.CompilerParams(vmem_limit_bytes=VMEM_BYTES),
        cost_estimate=pl.CostEstimate(flops=planes * wide * wide * size * 4, bytes_accessed=planes * wide * wide * 2, transcendentals=0),
        name="kernel_tables",
    )(w_kernels.reshape(planes, size, width), *constants)


def shards(vis_obs, uv_coords, vis_weight, block_group, tile_slot, w_plane, model_tiles, w_kernels):
    blocks, _, pols, vis_count = vis_obs.shape
    peers = lax.axis_size("peer")
    groups = 2 * peers
    owned = model_tiles.shape[0]
    tile_shape = model_tiles.shape[1:]
    flat_shape = (tile_shape[0] * tile_shape[1], tile_shape[2])
    capacity = max(2, 2 * blocks // groups)
    swap = [(0, 1), (1, 0)]
    cut = 3 * owned // 8
    mirrored_low = lax.ppermute(model_tiles[:cut], "half", swap)
    high_tiles, mirrored_low = lax.optimization_barrier((model_tiles[cut:], mirrored_low))
    mirrored_high = lax.ppermute(high_tiles, "half", swap)
    mirrored = jnp.concatenate([mirrored_low, mirrored_high], axis=0)

    target = block_group[:, 0]
    far = lax.rem(lax.div(target, peers) + lax.axis_index("half"), 2)
    peer = lax.rem(target, peers)
    holder = far * peers + peer
    markers = holder[:, None] == jnp.arange(groups, dtype=jnp.int32)[None, :]
    counts = markers.astype(jnp.int32)
    before = jnp.cumsum(counts, axis=0) - counts
    rank = jnp.sum(jnp.where(markers, before, 0), axis=1)
    ranks = rank[:, None] == jnp.arange(capacity, dtype=jnp.int32)[None, :]
    wanted = jnp.sum(
        jnp.where(markers[:, :, None] & ranks[:, None, :], (tile_slot + 1)[:, None, None], 0), axis=0
    ).astype(jnp.float32)
    own_weight = jnp.broadcast_to(jnp.sum(vis_weight)[None, None], (peers, 1))

    def exchange(operand):
        return lax.all_to_all(operand, "peer", split_axis=0, concat_axis=0, tiled=True)

    answers = exchange(jnp.concatenate([wanted[:peers], wanted[peers:], own_weight], axis=1))
    near_request = answers[:, :capacity].astype(jnp.int32) - 1
    far_request = answers[:, capacity : 2 * capacity].astype(jnp.int32) - 1
    half_weight = jnp.sum(answers[:, 2 * capacity]).reshape(1)
    weight_sum = half_weight + lax.ppermute(half_weight, "half", swap)
    scaling = blocks * groups * vis_count / weight_sum

    tables = kernel_tables(w_kernels, pols)
    near_count = blocks - jnp.sum(far)
    far_base = (near_count + BATCH - 1) // BATCH * BATCH
    item = jnp.where(far == 1, far_base + jnp.cumsum(far) - 1, jnp.cumsum(1 - far) - 1)
    items = jnp.arange(blocks + BATCH, dtype=jnp.int32)
    order = jnp.sum(
        jnp.where(items[:, None] == item[None, :], jnp.arange(blocks, dtype=jnp.int32)[None, :], 0), axis=1
    )
    slot = peer * capacity + rank
    u = jnp.take(uv_coords[:, 0], order, axis=0, mode="clip")
    v = jnp.take(uv_coords[:, 1], order, axis=0, mode="clip")
    weight = jnp.take(vis_weight, order, axis=0, mode="clip")

    def choose(tiles, request):
        chosen = jnp.take(tiles, jnp.maximum(request, 0).reshape(-1), axis=0, mode="clip")
        return chosen.reshape(request.shape + tile_shape)

    def send_tiles(chosen):
        return exchange(chosen).reshape((-1,) + tile_shape)

    def send_back(part):
        return exchange(part.reshape((peers, capacity) + part.shape[1:])).reshape((peers * capacity,) + part.shape[1:])

    near_request, mirrored_low = lax.optimization_barrier((near_request, mirrored_low))
    near_tiles = send_tiles(choose(model_tiles, near_request))
    chosen, order, slot, u, v, weight, tables = lax.optimization_barrier(
        (choose(mirrored, far_request), order, slot, u, v, weight, tables)
    )
    far_tiles = send_tiles(chosen)
    given = (vis_obs, u, v, weight, tables)
    zero = jnp.zeros((), jnp.int32)
    opening = max(BATCH, blocks // 4 // BATCH * BATCH)
    first_count = jnp.minimum(near_count, opening)
    residual, near_sent = process_blocks(opening, zero, first_count, order, slot, w_plane, near_tiles, *given)
    residual, far_sent = process_blocks(
        blocks, far_base, blocks - near_count, order, slot, w_plane, far_tiles, *given, (residual,)
    )
    far_sum = sum_tiles(
        far_request.reshape(-1), send_back(far_sent).reshape((-1,) + flat_shape), owned, jnp.bfloat16
    )
    relayed = lax.ppermute(far_sum, "half", swap)
    residual, near_sent = process_blocks(
        blocks - opening,
        zero + opening,
        near_count - first_count,
        order,
        slot,
        w_plane,
        near_tiles,
        *given,
        (residual, near_sent),
    )
    near_sent, far_sum = lax.optimization_barrier((near_sent, far_sum))
    returned = send_back(near_sent).reshape((-1,) + flat_shape)
    summed = sum_tiles(near_request.reshape(-1), returned, owned, jnp.float32, scaling, [relayed])
    return residual, summed.reshape(model_tiles.shape)


def solution(mesh):
    devices = mesh.devices.reshape(2, -1)
    halves = Mesh(devices, ("half", "peer"))
    rows = P(("half", "peer"))
    in_specs = (rows,) * 7 + (P(),)
    return jax.shard_map(shards, mesh=halves, in_specs=in_specs, out_specs=(rows, rows), check_vma=False)
```

```python
import functools
import math

import jax
import jax.numpy as jnp
import numpy as np
from jax import lax
from jax.experimental import pallas as pl
from jax.experimental.pallas import tpu as pltpu
from jax.sharding import Mesh
from jax.sharding import PartitionSpec as P

AXES = ("facet", "vis")
BATCH = 8
LANES = 512
TILE = 128
ROWS = 8
OPENING = 2
MIRROR_PARTS = (0, 3, 8)
UNROLL = 8
VMEM_BYTES = 60 * 1024 * 1024
SIN_TERMS = [(-1.0) ** i * (2.0 * math.pi) ** (2 * i + 1) / math.factorial(2 * i + 1) for i in range(8)]
COS_TERMS = [(-1.0) ** i * (2.0 * math.pi) ** (2 * i) / math.factorial(2 * i) for i in range(9)]


def polynomial(terms, square):
    total = jnp.full_like(square, terms[-1])
    for term in terms[-2::-1]:
        total = total * square + term
    return total


def unit_phasor(turns):
    halves = jnp.floor(turns * 2.0 + 0.5)
    part = turns - halves * 0.5
    odd = halves - 2.0 * jnp.floor(halves * 0.5)
    sign = 1.0 - 2.0 * odd
    square = part * part
    return sign * polynomial(COS_TERMS, square), -sign * part * polynomial(SIN_TERMS, square)


def phasor_powers(cosine, sine, count):
    powers = {1: (cosine, sine)}
    for j in range(2, count + 1):
        ar, ai = powers[j // 2]
        br, bi = powers[j - j // 2]
        if j % 2 == 0:
            powers[j] = (ar * ar - ai * ai, 2.0 * ar * ai)
        else:
            powers[j] = (ar * br - ai * bi, ar * bi + ai * br)
    return powers


def rows_dot(left, right, left_dim, right_dim):
    return lax.dot_general(
        left, right, (((left_dim,), (right_dim,)), ((), ())), preferred_element_type=jnp.float32
    )


def split(value):
    high = value.astype(jnp.bfloat16)
    return high, (value - high.astype(jnp.float32)).astype(jnp.bfloat16)


def block_kernel(
    meta, order, slot, plane, tiles, observed, u_ref, v_ref, w_ref, left_ref, back_ref, right_ref, turned_ref, *rest, carried
):
    res, con, fu_ref, fv_ref, tile_buf, obs_buf, model_buf, grid_buf, res_buf, con_buf, in_sems, out_sems = rest[carried:]
    quarter = fv_ref.shape[0] // 2 - 1
    half = 2 * quarter
    width = 2 * half
    pols = obs_buf.shape[3]
    span = pols * width
    vis_count = u_ref.shape[1]
    step = pl.program_id(0)
    base, count = meta[0], meta[1]

    def block_at(at, k):
        return order[base + jnp.minimum(at * BATCH + k, count - 1)]

    def incoming(at, k):
        block = block_at(at, k)
        turn = lax.rem(at, 2)
        return (
            pltpu.make_async_copy(tiles.at[slot[block]], tile_buf.at[turn, k], in_sems.at[0, turn, k]),
            pltpu.make_async_copy(observed.at[block], obs_buf.at[turn, k], in_sems.at[1, turn, k]),
        )

    def outgoing(at, k):
        block = block_at(at, k)
        return (
            pltpu.make_async_copy(con_buf.at[k], con.at[slot[block]], out_sems.at[0, k]),
            pltpu.make_async_copy(res_buf.at[k], res.at[block], out_sems.at[1, k]),
        )

    def start_incoming(at):
        for k in range(BATCH):
            for copy in incoming(at, k):
                copy.start()

    def make_phasors():
        cosine, sine = unit_phasor(u_ref[...] * (1.0 / width))
        powers = phasor_powers(cosine, sine, half)

        def put(row, value):
            for t in range(vis_count // TILE):
                fu_ref[t, row * BATCH : (row + 1) * BATCH, :] = value[:, t * TILE : (t + 1) * TILE]

        put(0, jnp.ones_like(cosine))
        put(half, powers[half][0])
        put(width, powers[half][1])
        for j in range(1, half):
            real, imag = powers[j]
            put(j, real)
            put(half + j, imag)
        for j in range(1, ROWS):
            put(width + j, jnp.zeros_like(cosine))
        cosine, sine = unit_phasor(v_ref[...] * (1.0 / width))
        powers = phasor_powers(cosine, sine, quarter)
        for j in range(1, quarter + 1):
            fv_ref[j], fv_ref[quarter + 1 + j] = powers[j]

    wide = 2 * span
    basis = 2 * (width + ROWS)
    lane = lax.broadcasted_iota(jnp.int32, (basis, span), 1)
    unpaired = lax.rem(lane, span // 2) < 2 * pols
    direct = lane < span // 2
    start_row = lax.broadcasted_iota(jnp.int32, (half, span), 0) == 0
    lone_row = start_row[:ROWS]

    def paired(full):
        other = jnp.roll(full, span // 2, axis=1)
        return jnp.where(unpaired, full, jnp.where(direct, full + other, other - full))

    def fold(full):
        total, change = full[:, :span] + full[:, span:], full[:, :span] - full[:, span:]

        def pairs(real, imag):
            ahead, behind = real[:half], real[half:]
            above, below = imag[:half], imag[half:]
            return [jnp.where(start_row, ahead, ahead + behind), jnp.where(start_row, behind, above - below)], (
                jnp.where(lone_row, -below[:ROWS], 0.0)
            )

        cos_pairs, cos_lone = pairs(total[:width], total[width:])
        sin_pairs, sin_lone = pairs(change[width:], -change[:width])
        return paired(jnp.concatenate(cos_pairs + sin_pairs + [cos_lone, sin_lone], axis=0))

    def unfold(sums):
        sums = paired(sums)
        cos_cos, sin_cos, cos_sin, sin_sin = [sums[i * half : (i + 1) * half] for i in range(4)]
        lone_cos = sums[4 * half :]
        lone_sin = jnp.concatenate([sums[4 * half + ROWS :]] * 2, axis=0)
        ahead = [cos_cos, jnp.where(start_row, 0.0, sin_cos), cos_sin, jnp.where(start_row, 0.0, sin_sin)]
        behind = [
            jnp.where(start_row, sin_cos, cos_cos),
            -jnp.where(start_row, lone_cos, sin_cos),
            jnp.where(start_row, sin_sin, cos_sin),
            -jnp.where(start_row, lone_sin, sin_sin),
        ]
        columns = []
        for side in (1.0, -1.0):
            rows = [[cc - side * ss, sc + side * cs] for cc, sc, cs, ss in (ahead, behind)]
            columns.append(jnp.concatenate([rows[0][0], rows[1][0], rows[0][1], rows[1][1]], axis=0))
        return jnp.concatenate(columns, axis=1)

    def from_right(which):
        band = lax.rem(lax.broadcasted_iota(jnp.int32, (width, wide), 1), pols)
        table = right_ref[which]
        zero = jnp.zeros((), jnp.bfloat16)
        return jnp.concatenate(
            [jnp.where(band == p, table[r * width : (r + 1) * width], zero) for r in range(2) for p in range(pols)],
            axis=0,
        )

    def make_model(k):
        which = plane[block_at(step, k)]
        tile = tile_buf[lax.rem(step, 2), k].reshape(2 * width, span)
        left = rows_dot(left_ref[which], tile, 1, 0).astype(jnp.bfloat16)
        left_real, left_imag = left[:width], left[width:]
        left = jnp.concatenate(
            [jnp.concatenate([left_real, left_imag], axis=1), jnp.concatenate([-left_imag, left_real], axis=1)],
            axis=0,
        )
        model_buf[k] = fold(rows_dot(left, from_right(which), 1, 0)).astype(jnp.bfloat16)

    turn = jnp.where(lax.broadcasted_iota(jnp.int32, (2 * pols, LANES), 0) < pols, -1.0, 1.0)

    def degrid_and_grid(k):
        model = model_buf[k]
        gridded = None
        for start in range(0, vis_count, LANES):
            lanes = pl.ds(start, LANES)
            along_u = jnp.concatenate(
                [
                    fu_ref[start // TILE + t, pl.ds(k, width + ROWS, stride=BATCH), :]
                    for t in range(LANES // TILE)
                ],
                axis=1,
            ).reshape((width + ROWS) // ROWS, ROWS, LANES)

            def phase(index):
                return jnp.broadcast_to(fv_ref[index, pl.ds(k, 1), lanes], (2 * pols, LANES))

            far_cos, far_sin = phase(quarter), phase(2 * quarter + 1)
            main, lone = along_u[: width // ROWS], along_u[width // ROWS :]
            along = jnp.concatenate([main * far_cos, main * far_sin, lone * far_cos, lone * far_sin], axis=0)
            along = along.reshape(basis, LANES).astype(jnp.bfloat16)
            spread = rows_dot(model, along, 0, 0).reshape(half, 2 * pols, LANES)
            cos_part = spread[0] + spread[quarter] * far_cos
            sin_part = -spread[quarter] * far_sin
            for j in range(1, quarter):
                cos_part = cos_part + spread[j] * phase(j)
                sin_part = sin_part + spread[quarter + j] * phase(quarter + 1 + j)
            predicted = cos_part + turn * jnp.roll(sin_part, pols, axis=0)
            given = obs_buf[lax.rem(step, 2), k, :, :, lanes]
            residual = jnp.concatenate([given[0], given[1]], axis=0) - predicted * (1.0 / width)
            res_buf[k, 0, :, lanes] = residual[:pols]
            res_buf[k, 1, :, lanes] = residual[pols:]
            scaled = residual * (w_ref[pl.ds(k, 1), lanes] * (1.0 / width))
            turned = -turn * jnp.roll(scaled, pols, axis=0)
            cos_rows, sin_rows = [scaled], [scaled * far_cos - turned * far_sin]
            for j in range(1, quarter):
                cos_rows.append(scaled * phase(j))
                sin_rows.append(turned * phase(quarter + 1 + j))
            weighted = jnp.concatenate(cos_rows + sin_rows, axis=0).astype(jnp.bfloat16)
            part = rows_dot(along, weighted, 1, 1)
            gridded = part if gridded is None else gridded + part
        grid_buf[k] = gridded

    def make_contribution(k):
        which = plane[block_at(step, k)]
        back = rows_dot(jnp.concatenate(split(unfold(grid_buf[k])), axis=0), turned_ref[which], 1, 0)
        back = back[: 2 * width] + back[2 * width :]
        back_real = back[:width, :span] + back[width:, span:]
        back_imag = back[:width, span:] - back[width:, :span]
        back = jnp.concatenate([back_real, back_imag], axis=0)
        result = rows_dot(back_ref[which], jnp.concatenate(split(back), axis=1), 1, 0)
        result = result[:, :span] + result[:, span:]
        con_buf[k] = result.astype(con_buf.dtype).reshape(con_buf.shape[1:])

    @pl.when(step * BATCH < count)
    def _():
        @pl.when(step == 0)
        def _():
            start_incoming(step)

        @pl.when((step + 1) * BATCH < count)
        def _():
            start_incoming(step + 1)

        make_phasors()
        for k in range(BATCH):
            for copy in incoming(step, k):
                copy.wait()
        for k in range(BATCH):
            make_model(k)

        @pl.when(step > 0)
        def _():
            for k in range(BATCH):
                for copy in outgoing(step - 1, k):
                    copy.wait()

        @pl.loop(0, BATCH // UNROLL)
        def _(i):
            for k in range(UNROLL):
                degrid_and_grid(i * UNROLL + k)

        for k in range(BATCH):
            make_contribution(k)
        last = (step + 1) * BATCH >= count
        for k in range(BATCH):

            @pl.when(step * BATCH + k < count)
            def _():
                for copy in outgoing(step, k):
                    copy.start()

        for k in range(BATCH):

            @pl.when(last & (step * BATCH + k < count))
            def _():
                for copy in outgoing(step, k):
                    copy.wait()


def process_blocks(most, base, count, order, slot, plane, tiles, observed, u, v, weight, tables, carried=()):
    pols, vis_count = observed.shape[2:]
    width = tiles.shape[2]
    meta = jnp.stack([base, count]).astype(jnp.int32)

    def by_batch(i, meta, order, slot, plane):
        return (lax.div(meta[0] + jnp.minimum(i * BATCH, jnp.maximum(meta[1] - 1, 0)), BATCH), 0)

    def whole(i, meta, order, slot, plane):
        return (0, 0, 0)

    row_spec = pl.BlockSpec((BATCH, vis_count), by_batch)
    hbm = pl.BlockSpec(memory_space=pl.ANY)
    operands = [tiles, observed, u, v, weight, *tables]
    in_specs = [hbm, hbm, row_spec, row_spec, row_spec] + [
        pl.BlockSpec(table.shape, whole) for table in tables
    ]
    aliases = {len(operands) + 4 + i: i for i in range(len(carried))}
    operands += carried
    in_specs += [hbm] * len(carried)
    tile_shape, vis_shape = tiles.shape[1:], observed.shape[1:]
    return pl.pallas_call(
        functools.partial(block_kernel, carried=len(carried)),
        out_shape=(
            jax.ShapeDtypeStruct(observed.shape, jnp.float32),
            jax.ShapeDtypeStruct(tiles.shape, jnp.bfloat16),
        ),
        grid_spec=pltpu.PrefetchScalarGridSpec(
            num_scalar_prefetch=4,
            grid=((most + BATCH - 1) // BATCH,),
            in_specs=in_specs,
            out_specs=(hbm, hbm),
            scratch_shapes=[
                pltpu.VMEM((vis_count // TILE, BATCH * (width + ROWS), TILE), jnp.float32),
                pltpu.VMEM((width // 2 + 2, BATCH, vis_count), jnp.float32),
                pltpu.VMEM((2, BATCH) + tile_shape, jnp.bfloat16),
                pltpu.VMEM((2, BATCH) + vis_shape, jnp.float32),
                pltpu.VMEM((BATCH, 2 * (width + ROWS), pols * width), jnp.bfloat16),
                pltpu.VMEM((BATCH, 2 * (width + ROWS), pols * width), jnp.float32),
                pltpu.VMEM((BATCH,) + vis_shape, jnp.float32),
                pltpu.VMEM((BATCH,) + tile_shape, jnp.bfloat16),
                pltpu.SemaphoreType.DMA((2, 2, BATCH)),
                pltpu.SemaphoreType.DMA((2, BATCH)),
            ],
        ),
        input_output_aliases=aliases,
        compiler_params=pltpu.CompilerParams(vmem_limit_bytes=VMEM_BYTES),
        cost_estimate=pl.CostEstimate(
            flops=most * 2 * 2 * 2 * width * 2 * pols * width * vis_count,
            bytes_accessed=most * 2 * pols * vis_count * 40,
            transcendentals=0,
        ),
        name="process_blocks",
    )(meta, order, slot, plane, *operands)


def sum_kernel(requested, scale_ref, *refs, last):
    if last:
        old_ref, arrived_ref, out_ref, total_ref = refs
        total_ref[: out_ref.shape[0]] = old_ref[...]
    else:
        arrived_ref, out_ref, total_ref = refs
        total_ref[...] = jnp.zeros_like(total_ref)
    unused = out_ref.shape[0]
    slots = arrived_ref.shape[0]
    together = math.gcd(slots, 8)

    @pl.loop(0, slots // together)
    def _(i):
        for k in range(together):
            at = i * together + k
            tile = requested[at]
            total_ref[jnp.where(tile < 0, unused, tile)] += arrived_ref[at].astype(jnp.float32)

    total = total_ref[:unused]
    out_ref[...] = total * scale_ref[0] if last else total


def sum_tiles(requested, scale, arrived, owned, old=None):
    shape = (owned,) + arrived.shape[1:]
    operands = [arrived] if old is None else [old, arrived]
    vmem = pl.BlockSpec(memory_space=pltpu.VMEM)
    return pl.pallas_call(
        functools.partial(sum_kernel, last=old is not None),
        out_shape=jax.ShapeDtypeStruct(shape, jnp.float32),
        in_specs=[pl.BlockSpec(memory_space=pltpu.SMEM)] * 2 + [vmem] * len(operands),
        out_specs=vmem,
        scratch_shapes=[pltpu.VMEM((owned + 1,) + shape[1:], jnp.float32)],
        compiler_params=pltpu.CompilerParams(vmem_limit_bytes=VMEM_BYTES),
        cost_estimate=pl.CostEstimate(flops=arrived.size, bytes_accessed=arrived.size * 4, transcendentals=0),
        name="sum_tiles",
    )(requested, scale, *operands)


def table_kernel(planes_ref, signs_ref, columns_ref, spread_ref, gather_ref, repeat_ref, left_ref, back_ref, right_ref, turned_ref):
    size = left_ref.shape[1]
    wide = right_ref.shape[2]
    pols = wide // size
    row = lax.rem(lax.broadcasted_iota(jnp.int32, (wide, wide), 0), pols)
    column = lax.rem(lax.div(lax.broadcasted_iota(jnp.int32, (wide, wide), 1), size // 2), pols)
    same = row == column
    zero = jnp.zeros((), jnp.bfloat16)

    def exact(left, right, left_dim=1):
        return rows_dot(left, right, left_dim, 0).astype(jnp.bfloat16)

    for k in range(planes_ref.shape[0]):
        def embed(signs):
            both = exact(signs, planes_ref[k])
            return jnp.concatenate([both[:size], both[size:]], axis=1)

        left = embed(signs_ref[...])
        left_ref[k] = left
        back = exact(left, jnp.eye(size, dtype=jnp.bfloat16), 0)
        back_ref[k] = back
        columns = embed(columns_ref[...])
        right_ref[k] = exact(columns, spread_ref[...], 0)
        turned_ref[k] = jnp.where(same, exact(exact(gather_ref[...], columns), repeat_ref[...]), zero)


def kernel_tables(w_kernels, pols):
    planes, _, width, _ = w_kernels.shape
    half = width // 2
    size, wide = 2 * width, 2 * width * pols


    def signs(offsets):
        pick = np.eye(width)[np.array(offsets) + half]
        none = np.zeros_like(pick)
        return np.block([[pick, none], [none, pick], [none, -pick], [pick, none]])

    def paired(count):
        return [*range(count), -count, *range(-1, -count, -1)]

    quarter = half // 2
    rows = signs(paired(half))
    columns = signs([c + side * quarter for side in (1, -1) for c in paired(quarter)])
    spread = np.zeros((2, width, width, 2, pols))
    repeat = np.zeros((2, width, 2, pols, width))
    for r in range(2):
        for n in range(width):
            spread[r, n, n, r] = 1.0
            repeat[r, n, r, :, n] = 1.0
    spread, repeat = spread.reshape(size, wide), repeat.reshape(size, wide)
    constants = [jnp.asarray(table, jnp.bfloat16) for table in (rows, columns, spread, spread.T, repeat)]
    part = math.gcd(planes, 8)

    def by_part(shape):
        return pl.BlockSpec((part,) + shape, lambda i: (i, 0, 0))

    shapes = [(size, size), (size, size), (size, wide), (wide, wide)]
    return pl.pallas_call(
        table_kernel,
        grid=(planes // part,),
        out_shape=[jax.ShapeDtypeStruct((planes,) + shape, jnp.bfloat16) for shape in shapes],
        in_specs=[by_part((size, width))] + [pl.BlockSpec(table.shape, lambda i: (0, 0)) for table in constants],
        out_specs=[by_part(shape) for shape in shapes],
        compiler_params=pltpu.CompilerParams(vmem_limit_bytes=VMEM_BYTES),
        cost_estimate=pl.CostEstimate(flops=planes * wide * wide * size * 4, bytes_accessed=planes * wide * wide * 2, transcendentals=0),
        name="kernel_tables",
    )(w_kernels.reshape(planes, size, width), *constants)


def exchange(operand):
    return lax.all_to_all(operand, AXES, split_axis=0, concat_axis=0, tiled=True)


def request_kernel(target_ref, slot_ref, weight_ref, out_ref, *, capacity):
    groups, lanes = out_ref.shape
    blocks = target_ref.shape[1]

    def iota(shape, dim):
        return lax.broadcasted_iota(jnp.int32, shape, dim)

    named = target_ref[...] == iota((groups, blocks), 0)
    named_bits = named.astype(jnp.float32).astype(jnp.bfloat16)
    ahead = (iota((blocks, blocks), 0) < iota((blocks, blocks), 1)).astype(jnp.float32).astype(jnp.bfloat16)
    before = rows_dot(named_bits, ahead, 1, 0)
    rank = jnp.sum(jnp.where(named, before, 0.0), axis=0, keepdims=True).astype(jnp.int32)
    asked = jnp.where(rank == iota((lanes, blocks), 0), slot_ref[...] + 1, 0)
    wanted = rows_dot(named_bits, asked.astype(jnp.float32).astype(jnp.bfloat16), 1, 1)
    weight = jnp.sum(weight_ref[...])
    out_ref[...] = jnp.where(iota((groups, lanes), 1) == capacity, weight, wanted)


def requests_of(target, tile_slot, vis_weight, groups, capacity):
    vmem = pl.BlockSpec(memory_space=pltpu.VMEM)
    return pl.pallas_call(
        functools.partial(request_kernel, capacity=capacity),
        out_shape=jax.ShapeDtypeStruct((groups, TILE), jnp.float32),
        in_specs=[vmem] * 3,
        out_specs=vmem,
        compiler_params=pltpu.CompilerParams(vmem_limit_bytes=VMEM_BYTES),
        name="requests_of",
    )(target.reshape(1, -1), tile_slot.reshape(1, -1), vis_weight)


def shards(vis_obs, uv_coords, vis_weight, block_group, tile_slot, w_plane, model_tiles, w_kernels):
    blocks = vis_obs.shape[0]
    pols = vis_obs.shape[2]
    groups = lax.axis_size(AXES)
    owned = model_tiles.shape[0]
    tile_shape = model_tiles.shape[1:]
    capacity = max(2, 2 * blocks // groups)
    early = max(1, 3 * capacity // 8)
    target = block_group[:, 0]
    markers = target[:, None] == jnp.arange(groups, dtype=jnp.int32)[None, :]
    counts = markers.astype(jnp.int32)
    before = jnp.cumsum(counts, axis=0) - counts
    rank = jnp.sum(jnp.where(markers, before, 0), axis=1)
    answers = exchange(requests_of(target, tile_slot, vis_weight, groups, capacity))
    requested = answers[:, :capacity].astype(jnp.int32) - 1
    weight_sum = jnp.sum(answers[:, capacity])
    scaling = blocks * groups * vis_obs.shape[-1] / weight_sum
    scaling = scaling.reshape(1)

    tables = kernel_tables(w_kernels, pols)
    is_late = rank >= early
    late = is_late.astype(jnp.int32)
    early_count = blocks - jnp.sum(late)
    late_base = (early_count + BATCH - 1) // BATCH * BATCH
    item = jnp.where(is_late, late_base + jnp.cumsum(late) - 1, jnp.cumsum(1 - late) - 1)
    items = jnp.arange(blocks + BATCH, dtype=jnp.int32)
    order = jnp.sum(
        jnp.where(items[:, None] == item[None, :], jnp.arange(blocks, dtype=jnp.int32)[None, :], 0), axis=1
    )
    slot = jnp.where(is_late, target * (capacity - early) + rank - early, target * early + rank)
    u = jnp.take(uv_coords[:, 0], order, axis=0, mode="clip")
    v = jnp.take(uv_coords[:, 1], order, axis=0, mode="clip")
    weight = jnp.take(vis_weight, order, axis=0, mode="clip")

    def choose(part):
        chosen = jnp.take(model_tiles, jnp.maximum(part, 0).reshape(-1), axis=0, mode="clip")
        return chosen.reshape(part.shape + tile_shape)

    def send_tiles(chosen):
        return exchange(chosen).reshape((-1,) + tile_shape)

    def send_back(part):
        returned = exchange(part.reshape((groups, -1) + tile_shape))
        return returned.reshape(-1, tile_shape[0] * tile_shape[1], tile_shape[2])

    first, second = requested[:, :early], requested[:, early:]
    tiles_first = send_tiles(choose(first))
    chosen, order, slot, u, v, weight, tables = lax.optimization_barrier(
        (choose(second), order, slot, u, v, weight, tables)
    )
    tiles_second = send_tiles(chosen)
    given = (vis_obs, u, v, weight, tables)
    zero = jnp.zeros((), jnp.int32)
    residual, sent_first = process_blocks(
        blocks, zero, early_count, order, slot, w_plane, tiles_first, *given
    )
    late_most = blocks * (capacity - early) // capacity
    residual, sent_second = process_blocks(
        late_most, late_base, blocks - early_count, order, slot, w_plane, tiles_second, *given, (residual,)
    )
    summed = sum_tiles(first.reshape(-1), scaling, send_back(sent_first), owned)
    summed = sum_tiles(second.reshape(-1), scaling, send_back(sent_second), owned, summed)
    return residual, summed.reshape(model_tiles.shape)


def solution(mesh):
    rows = P(AXES)
    in_specs = (rows,) * 7 + (P(),)
    return jax.shard_map(shards, mesh=mesh, in_specs=in_specs, out_specs=(rows, rows), check_vma=False)
```

```python
import functools
import math

import jax
import jax.numpy as jnp
import numpy as np
from jax import lax
from jax.experimental import pallas as pl
from jax.experimental.pallas import tpu as pltpu
from jax.sharding import Mesh
from jax.sharding import PartitionSpec as P

AXES = ("facet", "vis")
BATCH = 8
LANES = 512
TILE = 128
ROWS = 8
OPENING = 2
MIRROR_PARTS = (0, 3, 8)
UNROLL = 8
VMEM_BYTES = 60 * 1024 * 1024
SIN_TERMS = [(-1.0) ** i * (2.0 * math.pi) ** (2 * i + 1) / math.factorial(2 * i + 1) for i in range(8)]
COS_TERMS = [(-1.0) ** i * (2.0 * math.pi) ** (2 * i) / math.factorial(2 * i) for i in range(9)]


def polynomial(terms, square):
    total = jnp.full_like(square, terms[-1])
    for term in terms[-2::-1]:
        total = total * square + term
    return total


def unit_phasor(turns):
    halves = jnp.floor(turns * 2.0 + 0.5)
    part = turns - halves * 0.5
    odd = halves - 2.0 * jnp.floor(halves * 0.5)
    sign = 1.0 - 2.0 * odd
    square = part * part
    return sign * polynomial(COS_TERMS, square), -sign * part * polynomial(SIN_TERMS, square)


def phasor_powers(cosine, sine, count):
    powers = {1: (cosine, sine)}
    for j in range(2, count + 1):
        ar, ai = powers[j // 2]
        br, bi = powers[j - j // 2]
        if j % 2 == 0:
            powers[j] = (ar * ar - ai * ai, 2.0 * ar * ai)
        else:
            powers[j] = (ar * br - ai * bi, ar * bi + ai * br)
    return powers


def rows_dot(left, right, left_dim, right_dim):
    return lax.dot_general(
        left, right, (((left_dim,), (right_dim,)), ((), ())), preferred_element_type=jnp.float32
    )


def split(value):
    high = value.astype(jnp.bfloat16)
    return high, (value - high.astype(jnp.float32)).astype(jnp.bfloat16)


def block_kernel(
    meta, order, slot, plane, tiles, observed, u_ref, v_ref, w_ref, left_ref, back_ref, right_ref, turned_ref, *rest, carried
):
    res, con, fu_ref, fv_ref, tile_buf, obs_buf, model_buf, grid_buf, res_buf, con_buf, in_sems, out_sems = rest[carried:]
    quarter = fv_ref.shape[0] // 2 - 1
    half = 2 * quarter
    width = 2 * half
    pols = obs_buf.shape[3]
    span = pols * width
    vis_count = u_ref.shape[1]
    step = pl.program_id(0)
    base, count = meta[0], meta[1]

    def block_at(at, k):
        return order[base + jnp.minimum(at * BATCH + k, count - 1)]

    def incoming(at, k):
        block = block_at(at, k)
        turn = lax.rem(at, 2)
        return (
            pltpu.make_async_copy(tiles.at[slot[block]], tile_buf.at[turn, k], in_sems.at[0, turn, k]),
            pltpu.make_async_copy(observed.at[block], obs_buf.at[turn, k], in_sems.at[1, turn, k]),
        )

    def outgoing(at, k):
        block = block_at(at, k)
        return (
            pltpu.make_async_copy(con_buf.at[k], con.at[slot[block]], out_sems.at[0, k]),
            pltpu.make_async_copy(res_buf.at[k], res.at[block], out_sems.at[1, k]),
        )

    def start_incoming(at):
        for k in range(BATCH):
            for copy in incoming(at, k):
                copy.start()

    def make_phasors():
        cosine, sine = unit_phasor(u_ref[...] * (1.0 / width))
        powers = phasor_powers(cosine, sine, half)

        def put(row, value):
            for t in range(vis_count // TILE):
                fu_ref[t, row * BATCH : (row + 1) * BATCH, :] = value[:, t * TILE : (t + 1) * TILE]

        put(0, jnp.ones_like(cosine))
        put(half, powers[half][0])
        put(width, powers[half][1])
        for j in range(1, half):
            real, imag = powers[j]
            put(j, real)
            put(half + j, imag)
        for j in range(1, ROWS):
            put(width + j, jnp.zeros_like(cosine))
        cosine, sine = unit_phasor(v_ref[...] * (1.0 / width))
        powers = phasor_powers(cosine, sine, quarter)
        for j in range(1, quarter + 1):
            fv_ref[j], fv_ref[quarter + 1 + j] = powers[j]

    wide = 2 * span
    basis = 2 * (width + ROWS)
    lane = lax.broadcasted_iota(jnp.int32, (basis, span), 1)
    unpaired = lax.rem(lane, span // 2) < 2 * pols
    direct = lane < span // 2
    start_row = lax.broadcasted_iota(jnp.int32, (half, span), 0) == 0
    lone_row = start_row[:ROWS]

    def paired(full):
        other = jnp.roll(full, span // 2, axis=1)
        return jnp.where(unpaired, full, jnp.where(direct, full + other, other - full))

    def fold(full):
        total, change = full[:, :span] + full[:, span:], full[:, :span] - full[:, span:]

        def pairs(real, imag):
            ahead, behind = real[:half], real[half:]
            above, below = imag[:half], imag[half:]
            return [jnp.where(start_row, ahead, ahead + behind), jnp.where(start_row, behind, above - below)], (
                jnp.where(lone_row, -below[:ROWS], 0.0)
            )

        cos_pairs, cos_lone = pairs(total[:width], total[width:])
        sin_pairs, sin_lone = pairs(change[width:], -change[:width])
        return paired(jnp.concatenate(cos_pairs + sin_pairs + [cos_lone, sin_lone], axis=0))

    def unfold(sums):
        sums = paired(sums)
        cos_cos, sin_cos, cos_sin, sin_sin = [sums[i * half : (i + 1) * half] for i in range(4)]
        lone_cos = sums[4 * half :]
        lone_sin = jnp.concatenate([sums[4 * half + ROWS :]] * 2, axis=0)
        ahead = [cos_cos, jnp.where(start_row, 0.0, sin_cos), cos_sin, jnp.where(start_row, 0.0, sin_sin)]
        behind = [
            jnp.where(start_row, sin_cos, cos_cos),
            -jnp.where(start_row, lone_cos, sin_cos),
            jnp.where(start_row, sin_sin, cos_sin),
            -jnp.where(start_row, lone_sin, sin_sin),
        ]
        columns = []
        for side in (1.0, -1.0):
            rows = [[cc - side * ss, sc + side * cs] for cc, sc, cs, ss in (ahead, behind)]
            columns.append(jnp.concatenate([rows[0][0], rows[1][0], rows[0][1], rows[1][1]], axis=0))
        return jnp.concatenate(columns, axis=1)

    def from_right(which):
        band = lax.rem(lax.broadcasted_iota(jnp.int32, (width, wide), 1), pols)
        table = right_ref[which]
        zero = jnp.zeros((), jnp.bfloat16)
        return jnp.concatenate(
            [jnp.where(band == p, table[r * width : (r + 1) * width], zero) for r in range(2) for p in range(pols)],
            axis=0,
        )

    def make_model(k):
        which = plane[block_at(step, k)]
        tile = tile_buf[lax.rem(step, 2), k].reshape(2 * width, span)
        left = rows_dot(left_ref[which], tile, 1, 0).astype(jnp.bfloat16)
        left_real, left_imag = left[:width], left[width:]
        left = jnp.concatenate(
            [jnp.concatenate([left_real, left_imag], axis=1), jnp.concatenate([-left_imag, left_real], axis=1)],
            axis=0,
        )
        model_buf[k] = fold(rows_dot(left, from_right(which), 1, 0)).astype(jnp.bfloat16)

    turn = jnp.where(lax.broadcasted_iota(jnp.int32, (2 * pols, LANES), 0) < pols, -1.0, 1.0)

    def degrid_and_grid(k):
        model = model_buf[k]
        gridded = None
        for start in range(0, vis_count, LANES):
            lanes = pl.ds(start, LANES)
            along_u = jnp.concatenate(
                [
                    fu_ref[start // TILE + t, pl.ds(k, width + ROWS, stride=BATCH), :]
                    for t in range(LANES // TILE)
                ],
                axis=1,
            ).reshape((width + ROWS) // ROWS, ROWS, LANES)

            def phase(index):
                return jnp.broadcast_to(fv_ref[index, pl.ds(k, 1), lanes], (2 * pols, LANES))

            far_cos, far_sin = phase(quarter), phase(2 * quarter + 1)
            main, lone = along_u[: width // ROWS], along_u[width // ROWS :]
            along = jnp.concatenate([main * far_cos, main * far_sin, lone * far_cos, lone * far_sin], axis=0)
            along = along.reshape(basis, LANES).astype(jnp.bfloat16)
            spread = rows_dot(model, along, 0, 0).reshape(half, 2 * pols, LANES)
            cos_part = spread[0] + spread[quarter] * far_cos
            sin_part = -spread[quarter] * far_sin
            for j in range(1, quarter):
                cos_part = cos_part + spread[j] * phase(j)
                sin_part = sin_part + spread[quarter + j] * phase(quarter + 1 + j)
            predicted = cos_part + turn * jnp.roll(sin_part, pols, axis=0)
            given = obs_buf[lax.rem(step, 2), k, :, :, lanes]
            residual = jnp.concatenate([given[0], given[1]], axis=0) - predicted * (1.0 / width)
            res_buf[k, 0, :, lanes] = residual[:pols]
            res_buf[k, 1, :, lanes] = residual[pols:]
            scaled = residual * (w_ref[pl.ds(k, 1), lanes] * (1.0 / width))
            turned = -turn * jnp.roll(scaled, pols, axis=0)
            cos_rows, sin_rows = [scaled], [scaled * far_cos - turned * far_sin]
            for j in range(1, quarter):
                cos_rows.append(scaled * phase(j))
                sin_rows.append(turned * phase(quarter + 1 + j))
            weighted = jnp.concatenate(cos_rows + sin_rows, axis=0).astype(jnp.bfloat16)
            part = rows_dot(along, weighted, 1, 1)
            gridded = part if gridded is None else gridded + part
        grid_buf[k] = gridded

    def make_contribution(k):
        which = plane[block_at(step, k)]
        back = rows_dot(jnp.concatenate(split(unfold(grid_buf[k])), axis=0), turned_ref[which], 1, 0)
        back = back[: 2 * width] + back[2 * width :]
        back_real = back[:width, :span] + back[width:, span:]
        back_imag = back[:width, span:] - back[width:, :span]
        back = jnp.concatenate([back_real, back_imag], axis=0)
        result = rows_dot(back_ref[which], jnp.concatenate(split(back), axis=1), 1, 0)
        result = result[:, :span] + result[:, span:]
        con_buf[k] = result.astype(con_buf.dtype).reshape(con_buf.shape[1:])

    @pl.when(step * BATCH < count)
    def _():
        @pl.when(step == 0)
        def _():
            start_incoming(step)

        @pl.when((step + 1) * BATCH < count)
        def _():
            start_incoming(step + 1)

        make_phasors()
        for k in range(BATCH):
            for copy in incoming(step, k):
                copy.wait()
        for k in range(BATCH):
            make_model(k)

        @pl.when(step > 0)
        def _():
            for k in range(BATCH):
                for copy in outgoing(step - 1, k):
                    copy.wait()

        @pl.loop(0, BATCH // UNROLL)
        def _(i):
            for k in range(UNROLL):
                degrid_and_grid(i * UNROLL + k)

        for k in range(BATCH):
            make_contribution(k)
        last = (step + 1) * BATCH >= count
        for k in range(BATCH):

            @pl.when(step * BATCH + k < count)
            def _():
                for copy in outgoing(step, k):
                    copy.start()

        for k in range(BATCH):

            @pl.when(last & (step * BATCH + k < count))
            def _():
                for copy in outgoing(step, k):
                    copy.wait()


def process_blocks(most, base, count, order, slot, plane, tiles, observed, u, v, weight, tables, carried=()):
    pols, vis_count = observed.shape[2:]
    width = tiles.shape[2]
    meta = jnp.stack([base, count]).astype(jnp.int32)

    def by_batch(i, meta, order, slot, plane):
        return (lax.div(meta[0] + jnp.minimum(i * BATCH, jnp.maximum(meta[1] - 1, 0)), BATCH), 0)

    def whole(i, meta, order, slot, plane):
        return (0, 0, 0)

    row_spec = pl.BlockSpec((BATCH, vis_count), by_batch)
    hbm = pl.BlockSpec(memory_space=pl.ANY)
    operands = [tiles, observed, u, v, weight, *tables]
    in_specs = [hbm, hbm, row_spec, row_spec, row_spec] + [
        pl.BlockSpec(table.shape, whole) for table in tables
    ]
    aliases = {len(operands) + 4 + i: i for i in range(len(carried))}
    operands += carried
    in_specs += [hbm] * len(carried)
    tile_shape, vis_shape = tiles.shape[1:], observed.shape[1:]
    return pl.pallas_call(
        functools.partial(block_kernel, carried=len(carried)),
        out_shape=(
            jax.ShapeDtypeStruct(observed.shape, jnp.float32),
            jax.ShapeDtypeStruct(tiles.shape, jnp.bfloat16),
        ),
        grid_spec=pltpu.PrefetchScalarGridSpec(
            num_scalar_prefetch=4,
            grid=((most + BATCH - 1) // BATCH,),
            in_specs=in_specs,
            out_specs=(hbm, hbm),
            scratch_shapes=[
                pltpu.VMEM((vis_count // TILE, BATCH * (width + ROWS + 1), TILE), jnp.float32),
                pltpu.VMEM((width // 2 + 2, BATCH, vis_count), jnp.float32),
                pltpu.VMEM((2, BATCH) + tile_shape, jnp.bfloat16),
                pltpu.VMEM((2, BATCH) + vis_shape, jnp.float32),
                pltpu.VMEM((BATCH, 2 * (width + ROWS), pols * width), jnp.bfloat16),
                pltpu.VMEM((BATCH, 2 * (width + ROWS), pols * width), jnp.float32),
                pltpu.VMEM((BATCH,) + vis_shape, jnp.float32),
                pltpu.VMEM((BATCH,) + tile_shape, jnp.bfloat16),
                pltpu.SemaphoreType.DMA((2, 2, BATCH)),
                pltpu.SemaphoreType.DMA((2, BATCH)),
            ],
        ),
        input_output_aliases=aliases,
        compiler_params=pltpu.CompilerParams(vmem_limit_bytes=VMEM_BYTES),
        cost_estimate=pl.CostEstimate(
            flops=most * 2 * 2 * 2 * width * 2 * pols * width * vis_count,
            bytes_accessed=most * 2 * pols * vis_count * 40,
            transcendentals=0,
        ),
        name="process_blocks",
    )(meta, order, slot, plane, *operands)


def sum_kernel(requested, scale_ref, *refs, last):
    if last:
        old_ref, arrived_ref, out_ref, total_ref = refs
        total_ref[: out_ref.shape[0]] = old_ref[...]
    else:
        arrived_ref, out_ref, total_ref = refs
        total_ref[...] = jnp.zeros_like(total_ref)
    unused = out_ref.shape[0]
    slots = arrived_ref.shape[0]
    together = math.gcd(slots, 8)

    @pl.loop(0, slots // together)
    def _(i):
        for k in range(together):
            at = i * together + k
            tile = requested[at]
            total_ref[jnp.where(tile < 0, unused, tile)] += arrived_ref[at].astype(jnp.float32)

    total = total_ref[:unused]
    out_ref[...] = total * scale_ref[0] if last else total


def sum_tiles(requested, scale, arrived, owned, old=None):
    shape = (owned,) + arrived.shape[1:]
    operands = [arrived] if old is None else [old, arrived]
    vmem = pl.BlockSpec(memory_space=pltpu.VMEM)
    return pl.pallas_call(
        functools.partial(sum_kernel, last=old is not None),
        out_shape=jax.ShapeDtypeStruct(shape, jnp.float32),
        in_specs=[pl.BlockSpec(memory_space=pltpu.SMEM)] * 2 + [vmem] * len(operands),
        out_specs=vmem,
        scratch_shapes=[pltpu.VMEM((owned + 1,) + shape[1:], jnp.float32)],
        compiler_params=pltpu.CompilerParams(vmem_limit_bytes=VMEM_BYTES // 4),
        cost_estimate=pl.CostEstimate(flops=arrived.size, bytes_accessed=arrived.size * 4, transcendentals=0),
        name="sum_tiles",
    )(requested, scale, *operands)


def table_kernel(planes_ref, signs_ref, columns_ref, spread_ref, gather_ref, repeat_ref, left_ref, back_ref, right_ref, turned_ref):
    size = left_ref.shape[1]
    wide = right_ref.shape[2]
    pols = wide // size
    row = lax.rem(lax.broadcasted_iota(jnp.int32, (wide, wide), 0), pols)
    column = lax.rem(lax.div(lax.broadcasted_iota(jnp.int32, (wide, wide), 1), size // 2), pols)
    same = row == column
    zero = jnp.zeros((), jnp.bfloat16)

    def exact(left, right, left_dim=1):
        return rows_dot(left, right, left_dim, 0).astype(jnp.bfloat16)

    for k in range(planes_ref.shape[0]):
        def embed(signs):
            both = exact(signs, planes_ref[k])
            return jnp.concatenate([both[:size], both[size:]], axis=1)

        left = embed(signs_ref[...])
        left_ref[k] = left
        back = exact(left, jnp.eye(size, dtype=jnp.bfloat16), 0)
        back_ref[k] = back
        columns = embed(columns_ref[...])
        right_ref[k] = exact(columns, spread_ref[...], 0)
        turned_ref[k] = jnp.where(same, exact(exact(gather_ref[...], columns), repeat_ref[...]), zero)


def kernel_tables(w_kernels, pols):
    planes, _, width, _ = w_kernels.shape
    half = width // 2
    size, wide = 2 * width, 2 * width * pols


    def signs(offsets):
        pick = np.eye(width)[np.array(offsets) + half]
        none = np.zeros_like(pick)
        return np.block([[pick, none], [none, pick], [none, -pick], [pick, none]])

    def paired(count):
        return [*range(count), -count, *range(-1, -count, -1)]

    quarter = half // 2
    rows = signs(paired(half))
    columns = signs([c + side * quarter for side in (1, -1) for c in paired(quarter)])
    spread = np.zeros((2, width, width, 2, pols))
    repeat = np.zeros((2, width, 2, pols, width))
    for r in range(2):
        for n in range(width):
            spread[r, n, n, r] = 1.0
            repeat[r, n, r, :, n] = 1.0
    spread, repeat = spread.reshape(size, wide), repeat.reshape(size, wide)
    constants = [jnp.asarray(table, jnp.bfloat16) for table in (rows, columns, spread, spread.T, repeat)]
    part = math.gcd(planes, 8)

    def by_part(shape):
        return pl.BlockSpec((part,) + shape, lambda i: (i, 0, 0))

    shapes = [(size, size), (size, size), (size, wide), (wide, wide)]
    return pl.pallas_call(
        table_kernel,
        grid=(planes // part,),
        out_shape=[jax.ShapeDtypeStruct((planes,) + shape, jnp.bfloat16) for shape in shapes],
        in_specs=[by_part((size, width))] + [pl.BlockSpec(table.shape, lambda i: (0, 0)) for table in constants],
        out_specs=[by_part(shape) for shape in shapes],
        compiler_params=pltpu.CompilerParams(vmem_limit_bytes=VMEM_BYTES),
        cost_estimate=pl.CostEstimate(flops=planes * wide * wide * size * 4, bytes_accessed=planes * wide * wide * 2, transcendentals=0),
        name="kernel_tables",
    )(w_kernels.reshape(planes, size, width), *constants)


def exchange(operand):
    return lax.all_to_all(operand, AXES, split_axis=0, concat_axis=0, tiled=True)


def request_kernel(target_ref, slot_ref, weight_ref, out_ref, *, capacity):
    groups, lanes = out_ref.shape
    blocks = target_ref.shape[1]

    def iota(shape, dim):
        return lax.broadcasted_iota(jnp.int32, shape, dim)

    named = target_ref[...] == iota((groups, blocks), 0)
    named_bits = named.astype(jnp.float32).astype(jnp.bfloat16)
    ahead = (iota((blocks, blocks), 0) < iota((blocks, blocks), 1)).astype(jnp.float32).astype(jnp.bfloat16)
    before = rows_dot(named_bits, ahead, 1, 0)
    rank = jnp.sum(jnp.where(named, before, 0.0), axis=0, keepdims=True).astype(jnp.int32)
    asked = jnp.where(rank == iota((lanes, blocks), 0), slot_ref[...] + 1, 0)
    wanted = rows_dot(named_bits, asked.astype(jnp.float32).astype(jnp.bfloat16), 1, 1)
    weight = jnp.sum(weight_ref[...])
    out_ref[...] = jnp.where(iota((groups, lanes), 1) == capacity, weight, wanted)


def requests_of(target, tile_slot, vis_weight, groups, capacity):
    vmem = pl.BlockSpec(memory_space=pltpu.VMEM)
    return pl.pallas_call(
        functools.partial(request_kernel, capacity=capacity),
        out_shape=jax.ShapeDtypeStruct((groups, TILE), jnp.float32),
        in_specs=[vmem] * 3,
        out_specs=vmem,
        compiler_params=pltpu.CompilerParams(vmem_limit_bytes=VMEM_BYTES),
        name="requests_of",
    )(target.reshape(1, -1), tile_slot.reshape(1, -1), vis_weight)


def shards(vis_obs, uv_coords, vis_weight, block_group, tile_slot, w_plane, model_tiles, w_kernels):
    blocks = vis_obs.shape[0]
    pols = vis_obs.shape[2]
    groups = lax.axis_size(AXES)
    owned = model_tiles.shape[0]
    tile_shape = model_tiles.shape[1:]
    capacity = max(2, 2 * blocks // groups)
    early = max(1, 3 * capacity // 8)
    target = block_group[:, 0]
    markers = target[:, None] == jnp.arange(groups, dtype=jnp.int32)[None, :]
    counts = markers.astype(jnp.int32)
    before = jnp.cumsum(counts, axis=0) - counts
    rank = jnp.sum(jnp.where(markers, before, 0), axis=1)
    answers = exchange(requests_of(target, tile_slot, vis_weight, groups, capacity))
    requested = answers[:, :capacity].astype(jnp.int32) - 1
    weight_sum = jnp.sum(answers[:, capacity])
    scaling = blocks * groups * vis_obs.shape[-1] / weight_sum
    scaling = scaling.reshape(1)

    tables = kernel_tables(w_kernels, pols)
    is_late = rank >= early
    late = is_late.astype(jnp.int32)
    early_count = blocks - jnp.sum(late)
    late_base = (early_count + BATCH - 1) // BATCH * BATCH
    item = jnp.where(is_late, late_base + jnp.cumsum(late) - 1, jnp.cumsum(1 - late) - 1)
    items = jnp.arange(blocks + BATCH, dtype=jnp.int32)
    order = jnp.sum(
        jnp.where(items[:, None] == item[None, :], jnp.arange(blocks, dtype=jnp.int32)[None, :], 0), axis=1
    )
    slot = jnp.where(is_late, target * (capacity - early) + rank - early, target * early + rank)
    u = jnp.take(uv_coords[:, 0], order, axis=0, mode="clip")
    v = jnp.take(uv_coords[:, 1], order, axis=0, mode="clip")
    weight = jnp.take(vis_weight, order, axis=0, mode="clip")

    def choose(part):
        chosen = jnp.take(model_tiles, jnp.maximum(part, 0).reshape(-1), axis=0, mode="clip")
        return chosen.reshape(part.shape + tile_shape)

    def send_tiles(chosen):
        return exchange(chosen).reshape((-1,) + tile_shape)

    def send_back(part):
        returned = exchange(part.reshape((groups, -1) + tile_shape))
        return returned.reshape(-1, tile_shape[0] * tile_shape[1], tile_shape[2])

    first, second = requested[:, :early], requested[:, early:]
    tiles_first = send_tiles(choose(first))
    chosen, order, slot, u, v, weight, tables = lax.optimization_barrier(
        (choose(second), order, slot, u, v, weight, tables)
    )
    tiles_second = send_tiles(chosen)
    given = (vis_obs, u, v, weight, tables)
    zero = jnp.zeros((), jnp.int32)
    residual, sent_first = process_blocks(
        blocks, zero, early_count, order, slot, w_plane, tiles_first, *given
    )
    late_most = blocks * (capacity - early) // capacity
    residual, sent_second = process_blocks(
        late_most, late_base, blocks - early_count, order, slot, w_plane, tiles_second, *given, (residual,)
    )
    summed = sum_tiles(first.reshape(-1), scaling, send_back(sent_first), owned)
    summed = sum_tiles(second.reshape(-1), scaling, send_back(sent_second), owned, summed)
    return residual, summed.reshape(model_tiles.shape)


def solution(mesh):
    rows = P(AXES)
    in_specs = (rows,) * 7 + (P(),)
    return jax.shard_map(shards, mesh=mesh, in_specs=in_specs, out_specs=(rows, rows), check_vma=False)
```

```python
import functools
import math

import jax
import jax.numpy as jnp
import numpy as np
from jax import lax
from jax.experimental import pallas as pl
from jax.experimental.pallas import tpu as pltpu
from jax.sharding import Mesh
from jax.sharding import PartitionSpec as P

AXES = ("facet", "vis")
BATCH = 8
LANES = 512
TILE = 128
ROWS = 8
UNROLL = 8
VMEM_BYTES = 60 * 1024 * 1024
SIN_TERMS = [(-1.0) ** i * (2.0 * math.pi) ** (2 * i + 1) / math.factorial(2 * i + 1) for i in range(8)]
COS_TERMS = [(-1.0) ** i * (2.0 * math.pi) ** (2 * i) / math.factorial(2 * i) for i in range(9)]


def polynomial(terms, square):
    total = jnp.full_like(square, terms[-1])
    for term in terms[-2::-1]:
        total = total * square + term
    return total


def unit_phasor(turns):
    halves = jnp.floor(turns * 2.0 + 0.5)
    part = turns - halves * 0.5
    odd = halves - 2.0 * jnp.floor(halves * 0.5)
    sign = 1.0 - 2.0 * odd
    square = part * part
    return sign * polynomial(COS_TERMS, square), -sign * part * polynomial(SIN_TERMS, square)


def phasor_powers(cosine, sine, count):
    powers = {1: (cosine, sine)}
    for j in range(2, count + 1):
        ar, ai = powers[j // 2]
        br, bi = powers[j - j // 2]
        if j % 2 == 0:
            powers[j] = (ar * ar - ai * ai, 2.0 * ar * ai)
        else:
            powers[j] = (ar * br - ai * bi, ar * bi + ai * br)
    return powers


def rows_dot(left, right, left_dim, right_dim):
    return lax.dot_general(
        left, right, (((left_dim,), (right_dim,)), ((), ())), preferred_element_type=jnp.float32
    )


def split(value):
    high = value.astype(jnp.bfloat16)
    return high, (value - high.astype(jnp.float32)).astype(jnp.bfloat16)


def block_kernel(
    meta, order, slot, plane, tiles, observed, u_ref, v_ref, w_ref, left_ref, back_ref, right_ref, turned_ref, *rest, carried
):
    res, con, fu_ref, fv_ref, tile_buf, obs_buf, model_buf, grid_buf, res_buf, con_buf, in_sems, out_sems = rest[carried:]
    quarter = fv_ref.shape[0] // 2 - 1
    half = 2 * quarter
    width = 2 * half
    pols = obs_buf.shape[3]
    span = pols * width
    vis_count = u_ref.shape[1]
    step = pl.program_id(0)
    base, count = meta[0], meta[1]

    def block_at(at, k):
        return order[base + jnp.minimum(at * BATCH + k, count - 1)]

    def incoming(at, k):
        block = block_at(at, k)
        turn = lax.rem(at, 2)
        return (
            pltpu.make_async_copy(tiles.at[slot[block]], tile_buf.at[turn, k], in_sems.at[0, turn, k]),
            pltpu.make_async_copy(observed.at[block], obs_buf.at[turn, k], in_sems.at[1, turn, k]),
        )

    def outgoing(at, k):
        block = block_at(at, k)
        return (
            pltpu.make_async_copy(con_buf.at[k], con.at[slot[block]], out_sems.at[0, k]),
            pltpu.make_async_copy(res_buf.at[k], res.at[block], out_sems.at[1, k]),
        )

    def start_incoming(at):
        for k in range(BATCH):
            for copy in incoming(at, k):
                copy.start()

    def make_phasors():
        cosine, sine = unit_phasor(u_ref[...] * (1.0 / width))
        powers = phasor_powers(cosine, sine, half)

        def put(row, value):
            for t in range(vis_count // TILE):
                fu_ref[t, row * BATCH : (row + 1) * BATCH, :] = value[:, t * TILE : (t + 1) * TILE]

        put(0, jnp.ones_like(cosine))
        put(half, powers[half][0])
        put(width, powers[half][1])
        for j in range(1, half):
            real, imag = powers[j]
            put(j, real)
            put(half + j, imag)
        for j in range(1, ROWS):
            put(width + j, jnp.zeros_like(cosine))
        cosine, sine = unit_phasor(v_ref[...] * (1.0 / width))
        powers = phasor_powers(cosine, sine, quarter)
        for j in range(1, quarter + 1):
            fv_ref[j], fv_ref[quarter + 1 + j] = powers[j]

    wide = 2 * span
    basis = 2 * (width + ROWS)
    lane = lax.broadcasted_iota(jnp.int32, (basis, span), 1)
    unpaired = lax.rem(lane, span // 2) < 2 * pols
    direct = lane < span // 2
    start_row = lax.broadcasted_iota(jnp.int32, (half, span), 0) == 0
    lone_row = start_row[:ROWS]

    def paired(full):
        other = jnp.roll(full, span // 2, axis=1)
        return jnp.where(unpaired, full, jnp.where(direct, full + other, other - full))

    def fold(full):
        total, change = full[:, :span] + full[:, span:], full[:, :span] - full[:, span:]

        def pairs(real, imag):
            ahead, behind = real[:half], real[half:]
            above, below = imag[:half], imag[half:]
            return [jnp.where(start_row, ahead, ahead + behind), jnp.where(start_row, behind, above - below)], (
                jnp.where(lone_row, -below[:ROWS], 0.0)
            )

        cos_pairs, cos_lone = pairs(total[:width], total[width:])
        sin_pairs, sin_lone = pairs(change[width:], -change[:width])
        return paired(jnp.concatenate(cos_pairs + sin_pairs + [cos_lone, sin_lone], axis=0))

    def unfold(sums):
        sums = paired(sums)
        cos_cos, sin_cos, cos_sin, sin_sin = [sums[i * half : (i + 1) * half] for i in range(4)]
        lone_cos = sums[4 * half :]
        lone_sin = jnp.concatenate([sums[4 * half + ROWS :]] * 2, axis=0)
        ahead = [cos_cos, jnp.where(start_row, 0.0, sin_cos), cos_sin, jnp.where(start_row, 0.0, sin_sin)]
        behind = [
            jnp.where(start_row, sin_cos, cos_cos),
            -jnp.where(start_row, lone_cos, sin_cos),
            jnp.where(start_row, sin_sin, cos_sin),
            -jnp.where(start_row, lone_sin, sin_sin),
        ]
        columns = []
        for side in (1.0, -1.0):
            rows = [[cc - side * ss, sc + side * cs] for cc, sc, cs, ss in (ahead, behind)]
            columns.append(jnp.concatenate([rows[0][0], rows[1][0], rows[0][1], rows[1][1]], axis=0))
        return jnp.concatenate(columns, axis=1)

    def from_right(which):
        band = lax.rem(lax.broadcasted_iota(jnp.int32, (width, wide), 1), pols)
        table = right_ref[which]
        zero = jnp.zeros((), jnp.bfloat16)
        return jnp.concatenate(
            [jnp.where(band == p, table[r * width : (r + 1) * width], zero) for r in range(2) for p in range(pols)],
            axis=0,
        )

    def make_model(k):
        which = plane[block_at(step, k)]
        tile = tile_buf[lax.rem(step, 2), k].reshape(2 * width, span)
        left = rows_dot(left_ref[which], tile, 1, 0).astype(jnp.bfloat16)
        left_real, left_imag = left[:width], left[width:]
        left = jnp.concatenate(
            [jnp.concatenate([left_real, left_imag], axis=1), jnp.concatenate([-left_imag, left_real], axis=1)],
            axis=0,
        )
        model_buf[k] = fold(rows_dot(left, from_right(which), 1, 0)).astype(jnp.bfloat16)

    turn = jnp.where(lax.broadcasted_iota(jnp.int32, (2 * pols, LANES), 0) < pols, -1.0, 1.0)

    def degrid_and_grid(k):
        model = model_buf[k]
        gridded = None
        for start in range(0, vis_count, LANES):
            lanes = pl.ds(start, LANES)
            along_u = jnp.concatenate(
                [
                    fu_ref[start // TILE + t, pl.ds(k, width + ROWS, stride=BATCH), :]
                    for t in range(LANES // TILE)
                ],
                axis=1,
            ).reshape((width + ROWS) // ROWS, ROWS, LANES)

            def phase(index):
                return jnp.broadcast_to(fv_ref[index, pl.ds(k, 1), lanes], (2 * pols, LANES))

            far_cos, far_sin = phase(quarter), phase(2 * quarter + 1)
            main, lone = along_u[: width // ROWS], along_u[width // ROWS :]
            along = jnp.concatenate([main * far_cos, main * far_sin, lone * far_cos, lone * far_sin], axis=0)
            along = along.reshape(basis, LANES).astype(jnp.bfloat16)
            spread = rows_dot(model, along, 0, 0).reshape(half, 2 * pols, LANES)
            cos_part = spread[0] + spread[quarter] * far_cos
            sin_part = -spread[quarter] * far_sin
            for j in range(1, quarter):
                cos_part = cos_part + spread[j] * phase(j)
                sin_part = sin_part + spread[quarter + j] * phase(quarter + 1 + j)
            predicted = cos_part + turn * jnp.roll(sin_part, pols, axis=0)
            given = obs_buf[lax.rem(step, 2), k, :, :, lanes]
            residual = jnp.concatenate([given[0], given[1]], axis=0) - predicted * (1.0 / width)
            res_buf[k, 0, :, lanes] = residual[:pols]
            res_buf[k, 1, :, lanes] = residual[pols:]
            scaled = residual * (w_ref[pl.ds(k, 1), lanes] * (1.0 / width))
            turned = -turn * jnp.roll(scaled, pols, axis=0)
            cos_rows, sin_rows = [scaled], [scaled * far_cos - turned * far_sin]
            for j in range(1, quarter):
                cos_rows.append(scaled * phase(j))
                sin_rows.append(turned * phase(quarter + 1 + j))
            weighted = jnp.concatenate(cos_rows + sin_rows, axis=0).astype(jnp.bfloat16)
            part = rows_dot(along, weighted, 1, 1)
            gridded = part if gridded is None else gridded + part
        grid_buf[k] = gridded

    def make_contribution(k):
        which = plane[block_at(step, k)]
        back = rows_dot(jnp.concatenate(split(unfold(grid_buf[k])), axis=0), turned_ref[which], 1, 0)
        back = back[: 2 * width] + back[2 * width :]
        back_real = back[:width, :span] + back[width:, span:]
        back_imag = back[:width, span:] - back[width:, :span]
        back = jnp.concatenate([back_real, back_imag], axis=0)
        result = rows_dot(back_ref[which], jnp.concatenate(split(back), axis=1), 1, 0)
        result = result[:, :span] + result[:, span:]
        con_buf[k] = result.astype(con_buf.dtype).reshape(con_buf.shape[1:])

    @pl.when(step * BATCH < count)
    def _():
        @pl.when(step == 0)
        def _():
            start_incoming(step)

        @pl.when((step + 1) * BATCH < count)
        def _():
            start_incoming(step + 1)

        make_phasors()
        for k in range(BATCH):
            for copy in incoming(step, k):
                copy.wait()
        for k in range(BATCH):
            make_model(k)

        @pl.when(step > 0)
        def _():
            for k in range(BATCH):
                for copy in outgoing(step - 1, k):
                    copy.wait()

        @pl.loop(0, BATCH // UNROLL)
        def _(i):
            for k in range(UNROLL):
                degrid_and_grid(i * UNROLL + k)

        for k in range(BATCH):
            make_contribution(k)
        last = (step + 1) * BATCH >= count
        for k in range(BATCH):

            @pl.when(step * BATCH + k < count)
            def _():
                for copy in outgoing(step, k):
                    copy.start()

        for k in range(BATCH):

            @pl.when(last & (step * BATCH + k < count))
            def _():
                for copy in outgoing(step, k):
                    copy.wait()


def process_blocks(most, base, count, order, slot, plane, tiles, observed, u, v, weight, tables, carried=()):
    pols, vis_count = observed.shape[2:]
    width = tiles.shape[2]
    meta = jnp.stack([base, count]).astype(jnp.int32)

    def by_batch(i, meta, order, slot, plane):
        return (lax.div(meta[0] + jnp.minimum(i * BATCH, jnp.maximum(meta[1] - 1, 0)), BATCH), 0)

    def whole(i, meta, order, slot, plane):
        return (0, 0, 0)

    row_spec = pl.BlockSpec((BATCH, vis_count), by_batch)
    hbm = pl.BlockSpec(memory_space=pl.ANY)
    operands = [tiles, observed, u, v, weight, *tables]
    in_specs = [hbm, hbm, row_spec, row_spec, row_spec] + [
        pl.BlockSpec(table.shape, whole) for table in tables
    ]
    aliases = {len(operands) + 4 + i: i for i in range(len(carried))}
    operands += carried
    in_specs += [hbm] * len(carried)
    tile_shape, vis_shape = tiles.shape[1:], observed.shape[1:]
    return pl.pallas_call(
        functools.partial(block_kernel, carried=len(carried)),
        out_shape=(
            jax.ShapeDtypeStruct(observed.shape, jnp.float32),
            jax.ShapeDtypeStruct(tiles.shape, jnp.bfloat16),
        ),
        grid_spec=pltpu.PrefetchScalarGridSpec(
            num_scalar_prefetch=4,
            grid=((most + BATCH - 1) // BATCH,),
            in_specs=in_specs,
            out_specs=(hbm, hbm),
            scratch_shapes=[
                pltpu.VMEM((vis_count // TILE, BATCH * (width + ROWS + 1), TILE), jnp.float32),
                pltpu.VMEM((width // 2 + 2, BATCH, vis_count), jnp.float32),
                pltpu.VMEM((2, BATCH) + tile_shape, jnp.bfloat16),
                pltpu.VMEM((2, BATCH) + vis_shape, jnp.float32),
                pltpu.VMEM((BATCH, 2 * (width + ROWS), pols * width), jnp.bfloat16),
                pltpu.VMEM((BATCH, 2 * (width + ROWS), pols * width), jnp.float32),
                pltpu.VMEM((BATCH,) + vis_shape, jnp.float32),
                pltpu.VMEM((BATCH,) + tile_shape, jnp.bfloat16),
                pltpu.SemaphoreType.DMA((2, 2, BATCH)),
                pltpu.SemaphoreType.DMA((2, BATCH)),
            ],
        ),
        input_output_aliases=aliases,
        compiler_params=pltpu.CompilerParams(vmem_limit_bytes=VMEM_BYTES),
        cost_estimate=pl.CostEstimate(
            flops=most * 2 * 2 * 2 * width * 2 * pols * width * vis_count,
            bytes_accessed=most * 2 * pols * vis_count * 40,
            transcendentals=0,
        ),
        name="process_blocks",
    )(meta, order, slot, plane, *operands)


def sum_kernel(requested, scale_ref, *refs, last):
    if last:
        old, arrived, out, total_ref, other_ref, arrived_ref, out_ref, old_ref, in_sems, out_sems, old_sem = refs
        old_copy = pltpu.make_async_copy(old, old_ref, old_sem)
    else:
        arrived, out, total_ref, other_ref, arrived_ref, out_ref, in_sems, out_sems = refs
    unused = out.shape[0]
    parts = in_sems.shape[0]
    slots = arrived.shape[0] // parts
    tiles = unused // out_sems.shape[0]
    together = math.gcd(slots, 8) // 2
    copies = []
    for part in range(parts):
        rows = pl.ds(part * slots, slots)
        copies.append(pltpu.make_async_copy(arrived.at[rows], arrived_ref.at[rows], in_sems.at[part]))
        copies[part].start()
    if last:
        old_copy.start()
    total_ref[...] = jnp.zeros_like(total_ref)
    other_ref[...] = jnp.zeros_like(other_ref)

    for part in range(parts):
        copies[part].wait()

        @pl.loop(0, slots // (2 * together))
        def _(i):
            for k in range(together):
                at = part * slots + 2 * (i * together + k)
                tile, other = requested[at], requested[at + 1]
                tile, other = jnp.where(tile < 0, unused, tile), jnp.where(other < 0, unused, other)
                value = total_ref[tile] + arrived_ref[at].astype(jnp.float32)
                beside = other_ref[other] + arrived_ref[at + 1].astype(jnp.float32)
                total_ref[tile] = value
                other_ref[other] = beside

    if last:
        old_copy.wait()
    sent = []
    for part in range(out_sems.shape[0]):
        rows = pl.ds(part * tiles, tiles)
        total = total_ref[rows] + other_ref[rows]
        out_ref[rows] = (total + old_ref[rows]) * scale_ref[0] if last else total
        sent.append(pltpu.make_async_copy(out_ref.at[rows], out.at[rows], out_sems.at[part]))
        sent[part].start()
    for copy in sent:
        copy.wait()


def sum_tiles(requested, scale, arrived, owned, old=None):
    shape = (owned,) + arrived.shape[1:]
    last = old is not None
    operands = [old, arrived] if last else [arrived]
    scratch = [
        pltpu.VMEM((owned + 1,) + shape[1:], jnp.float32),
        pltpu.VMEM((owned + 1,) + shape[1:], jnp.float32),
        pltpu.VMEM(arrived.shape, arrived.dtype),
        pltpu.VMEM(shape, jnp.float32),
    ]
    sems = [pltpu.SemaphoreType.DMA((math.gcd(arrived.shape[0], 4),)), pltpu.SemaphoreType.DMA((math.gcd(owned, 4),))]
    if last:
        scratch.append(pltpu.VMEM(shape, jnp.float32))
        sems.append(pltpu.SemaphoreType.DMA(()))
    return pl.pallas_call(
        functools.partial(sum_kernel, last=last),
        out_shape=jax.ShapeDtypeStruct(shape, jnp.float32),
        in_specs=[pl.BlockSpec(memory_space=pltpu.SMEM)] * 2 + [pl.BlockSpec(memory_space=pl.ANY)] * len(operands),
        out_specs=pl.BlockSpec(memory_space=pl.ANY),
        scratch_shapes=scratch + sems,
        compiler_params=pltpu.CompilerParams(vmem_limit_bytes=VMEM_BYTES // 3),
        cost_estimate=pl.CostEstimate(flops=arrived.size, bytes_accessed=arrived.size * 4, transcendentals=0),
        name="sum_tiles",
    )(requested, scale, *operands)


def table_kernel(planes_ref, signs_ref, columns_ref, spread_ref, gather_ref, repeat_ref, left_ref, back_ref, right_ref, turned_ref):
    size = left_ref.shape[1]
    wide = right_ref.shape[2]
    pols = wide // size
    row = lax.rem(lax.broadcasted_iota(jnp.int32, (wide, wide), 0), pols)
    column = lax.rem(lax.div(lax.broadcasted_iota(jnp.int32, (wide, wide), 1), size // 2), pols)
    same = row == column
    zero = jnp.zeros((), jnp.bfloat16)

    def exact(left, right, left_dim=1):
        return rows_dot(left, right, left_dim, 0).astype(jnp.bfloat16)

    for k in range(planes_ref.shape[0]):
        def embed(signs):
            both = exact(signs, planes_ref[k])
            return jnp.concatenate([both[:size], both[size:]], axis=1)

        left = embed(signs_ref[...])
        left_ref[k] = left
        back = exact(left, jnp.eye(size, dtype=jnp.bfloat16), 0)
        back_ref[k] = back
        columns = embed(columns_ref[...])
        right_ref[k] = exact(columns, spread_ref[...], 0)
        turned_ref[k] = jnp.where(same, exact(exact(gather_ref[...], columns), repeat_ref[...]), zero)


def kernel_tables(w_kernels, pols):
    planes, _, width, _ = w_kernels.shape
    half = width // 2
    size, wide = 2 * width, 2 * width * pols


    def signs(offsets):
        pick = np.eye(width)[np.array(offsets) + half]
        none = np.zeros_like(pick)
        return np.block([[pick, none], [none, pick], [none, -pick], [pick, none]])

    def paired(count):
        return [*range(count), -count, *range(-1, -count, -1)]

    quarter = half // 2
    rows = signs(paired(half))
    columns = signs([c + side * quarter for side in (1, -1) for c in paired(quarter)])
    spread = np.zeros((2, width, width, 2, pols))
    repeat = np.zeros((2, width, 2, pols, width))
    for r in range(2):
        for n in range(width):
            spread[r, n, n, r] = 1.0
            repeat[r, n, r, :, n] = 1.0
    spread, repeat = spread.reshape(size, wide), repeat.reshape(size, wide)
    constants = [jnp.asarray(table, jnp.bfloat16) for table in (rows, columns, spread, spread.T, repeat)]
    part = math.gcd(planes, 8)

    def by_part(shape):
        return pl.BlockSpec((part,) + shape, lambda i: (i, 0, 0))

    shapes = [(size, size), (size, size), (size, wide), (wide, wide)]
    return pl.pallas_call(
        table_kernel,
        grid=(planes // part,),
        out_shape=[jax.ShapeDtypeStruct((planes,) + shape, jnp.bfloat16) for shape in shapes],
        in_specs=[by_part((size, width))] + [pl.BlockSpec(table.shape, lambda i: (0, 0)) for table in constants],
        out_specs=[by_part(shape) for shape in shapes],
        compiler_params=pltpu.CompilerParams(vmem_limit_bytes=VMEM_BYTES),
        cost_estimate=pl.CostEstimate(flops=planes * wide * wide * size * 4, bytes_accessed=planes * wide * wide * 2, transcendentals=0),
        name="kernel_tables",
    )(w_kernels.reshape(planes, size, width), *constants)


def exchange(operand):
    return lax.all_to_all(operand, AXES, split_axis=0, concat_axis=0, tiled=True)


def request_kernel(target_ref, slot_ref, weight_ref, out_ref, *, capacity):
    groups, lanes = out_ref.shape
    blocks = target_ref.shape[1]

    def iota(shape, dim):
        return lax.broadcasted_iota(jnp.int32, shape, dim)

    named = target_ref[...] == iota((groups, blocks), 0)
    named_bits = named.astype(jnp.float32).astype(jnp.bfloat16)
    ahead = (iota((blocks, blocks), 0) < iota((blocks, blocks), 1)).astype(jnp.float32).astype(jnp.bfloat16)
    before = rows_dot(named_bits, ahead, 1, 0)
    rank = jnp.sum(jnp.where(named, before, 0.0), axis=0, keepdims=True).astype(jnp.int32)
    asked = jnp.where(rank == iota((lanes, blocks), 0), slot_ref[...] + 1, 0)
    wanted = rows_dot(named_bits, asked.astype(jnp.float32).astype(jnp.bfloat16), 1, 1)
    weight = jnp.sum(weight_ref[...])
    out_ref[...] = jnp.where(iota((groups, lanes), 1) == capacity, weight, wanted)


def requests_of(target, tile_slot, vis_weight, groups, capacity):
    vmem = pl.BlockSpec(memory_space=pltpu.VMEM)
    return pl.pallas_call(
        functools.partial(request_kernel, capacity=capacity),
        out_shape=jax.ShapeDtypeStruct((groups, TILE), jnp.float32),
        in_specs=[vmem] * 3,
        out_specs=vmem,
        compiler_params=pltpu.CompilerParams(vmem_limit_bytes=VMEM_BYTES),
        name="requests_of",
    )(target.reshape(1, -1), tile_slot.reshape(1, -1), vis_weight)


def shards(vis_obs, uv_coords, vis_weight, block_group, tile_slot, w_plane, model_tiles, w_kernels):
    blocks = vis_obs.shape[0]
    pols = vis_obs.shape[2]
    groups = lax.axis_size(AXES)
    owned = model_tiles.shape[0]
    tile_shape = model_tiles.shape[1:]
    capacity = max(2, 2 * blocks // groups)
    early = max(1, 3 * capacity // 8)
    target = block_group[:, 0]
    markers = target[:, None] == jnp.arange(groups, dtype=jnp.int32)[None, :]
    counts = markers.astype(jnp.int32)
    before = jnp.cumsum(counts, axis=0) - counts
    rank = jnp.sum(jnp.where(markers, before, 0), axis=1)
    answers = exchange(requests_of(target, tile_slot, vis_weight, groups, capacity))
    requested = answers[:, :capacity].astype(jnp.int32) - 1
    weight_sum = jnp.sum(answers[:, capacity])
    scaling = blocks * groups * vis_obs.shape[-1] / weight_sum
    scaling = scaling.reshape(1)

    tables = kernel_tables(w_kernels, pols)
    is_late = rank >= early
    late = is_late.astype(jnp.int32)
    early_count = blocks - jnp.sum(late)
    late_base = (early_count + BATCH - 1) // BATCH * BATCH
    item = jnp.where(is_late, late_base + jnp.cumsum(late) - 1, jnp.cumsum(1 - late) - 1)
    items = jnp.arange(blocks + BATCH, dtype=jnp.int32)
    order = jnp.sum(
        jnp.where(items[:, None] == item[None, :], jnp.arange(blocks, dtype=jnp.int32)[None, :], 0), axis=1
    )
    slot = jnp.where(is_late, target * (capacity - early) + rank - early, target * early + rank)
    u = jnp.take(uv_coords[:, 0], order, axis=0, mode="clip")
    v = jnp.take(uv_coords[:, 1], order, axis=0, mode="clip")
    weight = jnp.take(vis_weight, order, axis=0, mode="clip")

    def choose(part):
        chosen = jnp.take(model_tiles, jnp.maximum(part, 0).reshape(-1), axis=0, mode="clip")
        return chosen.reshape(part.shape + tile_shape)

    def send_tiles(chosen):
        return exchange(chosen).reshape((-1,) + tile_shape)

    def send_back(part):
        returned = exchange(part.reshape((groups, -1) + tile_shape))
        return returned.reshape(-1, tile_shape[0] * tile_shape[1], tile_shape[2])

    first, second = requested[:, :early], requested[:, early:]
    tiles_first = send_tiles(choose(first))
    chosen, order, slot, u, v, weight, tables = lax.optimization_barrier(
        (choose(second), order, slot, u, v, weight, tables)
    )
    tiles_second = send_tiles(chosen)
    given = (vis_obs, u, v, weight, tables)
    zero = jnp.zeros((), jnp.int32)
    residual, sent_first = process_blocks(
        blocks, zero, early_count, order, slot, w_plane, tiles_first, *given
    )
    late_most = blocks * (capacity - early) // capacity
    residual, sent_second = process_blocks(
        late_most, late_base, blocks - early_count, order, slot, w_plane, tiles_second, *given, (residual,)
    )
    summed = sum_tiles(first.reshape(-1), scaling, send_back(sent_first), owned)
    summed = sum_tiles(second.reshape(-1), scaling, send_back(sent_second), owned, summed)
    return residual, summed.reshape(model_tiles.shape)


def solution(mesh):
    rows = P(AXES)
    in_specs = (rows,) * 7 + (P(),)
    return jax.shard_map(shards, mesh=mesh, in_specs=in_specs, out_specs=(rows, rows), check_vma=False)
```
